32 devices in a mesh: seq: 8 (over z, x), grp: 4 (over y, core).
Axes of the slice: x: 2, y: 2, z: 4, core: 2. Of those that a mesh axis runs over, the one named last changes fastest.
Arguments:
- queries: bfloat16 [4, 128, 4096], P('grp', 'seq'), may hold values from -200 to 200
- prefix_keys: bfloat16 [4, 8192, 512], P('grp', 'seq'), may hold values from -20 to 20
- prefix_values: bfloat16 [4, 8192, 512], P('grp', 'seq'), may hold values from -6 to 6
- suffix_keys: bfloat16 [4, 128, 512], P('grp', 'seq'), may hold values from -48 to 48
- suffix_values: bfloat16 [4, 128, 512], P('grp', 'seq'), may hold values from -6 to 6
- parents: int32 [4, 128], P('grp'), may hold values from 0 to 127, as said below
- out_proj: bfloat16 [4096, 4096], P('seq'), may hold values from -0.09375 to 0.09375
- residual: bfloat16 [4, 128, 4096], P('grp', 'seq'), may hold values from -6 to 6
- norm_gain: float32 [4096], replicated, may hold values from 0.5 to 1.5
- router: bfloat16 [4096, 32], replicated, may hold values from -0.09375 to 0.09375
- routes: int32 [4, 128, 8], P('grp', 'seq'), may hold values from 0 to 31, all different within a row; in each aligned block of 16 rows (0 to 15, 16 to 31, ..., all dimensions but the last counted through in order) at most 8 rows name the same one
- expert_gate: bfloat16 [32, 4096, 768], P(('seq', 'grp')), may hold values from -0.09375 to 0.09375
- expert_up: bfloat16 [32, 4096, 768], P(('seq', 'grp')), may hold values from -0.09375 to 0.09375
- expert_down: bfloat16 [32, 768, 4096], P(('seq', 'grp')), may hold values from -0.21875 to 0.21875
Outputs:
- layer_out: bfloat16 [4, 128, 4096], P('grp', 'seq')
The draws below stay inside these ranges and needn't reach their ends.
Inputs may be any that keep to these rules, and one draw needn't show every extreme that they name: Each request's rows form a forest of 8 levels, each a run of 16 rows: rows of the first level are their own parents; any other row's parent is a row of the level just before its own. `routes`: among the rows of one device no expert is named more than 8 times.
All inputs are finite; a program needn't handle non-finite values.
Results may differ from the reference program's by a relative error of at most 0.012.
Values may be sent and summed in bfloat16 or wider, within the bound.
A program may use at most 128 MiB of HBM per device.

```python
import math
import jax
import jax.numpy as jnp
import numpy as np
from jax import lax

D = 4096
HEADS = 32
KVH = 4
HD = 128
EFF = 768
TOP = 8
DEPTH = 8
ROWS_DEV = 16
R = 128
PREFIX = 8192
REQUESTS = 4
EXPERTS = 32
CAP = 8
N_SEQ = 8
N_GRP = 4


def prefix_base(key):
    base = jax.random.normal(jax.random.fold_in(key, 11), (REQUESTS, PREFIX, KVH * HD), jnp.float32)
    base = jnp.clip(base, -5.0, 5.0)
    position = jnp.arange(PREFIX, dtype=jnp.float32)[None, :, None] / PREFIX
    keys = base * (2.5 + position)
    return keys


def draw_prefix_keys(key, part):
    return prefix_base(key).astype(jnp.bfloat16)


def draw_queries(key, part):
    own_key = jax.random.fold_in(key, 12)
    shape = (REQUESTS, R, HEADS * HD)
    values = jnp.clip(jax.random.normal(own_key, shape, jnp.float32), -6.0, 6.0)
    return values.astype(jnp.bfloat16)


def draw_parents(key, part):
    level_size = R // DEPTH
    row = jnp.arange(R, dtype=jnp.int32)
    level = row // level_size
    offset = jax.random.randint(jax.random.fold_in(key, 21), (REQUESTS, R), 0, level_size, dtype=jnp.int32)
    parent = (level[None, :] - 1) * level_size + offset
    return jnp.where(level[None, :] == 0, row[None, :], parent).astype(jnp.int32)


def shard_levels(key, extent, cuts, least, largest):
    factor_of = 1.0
    for dim, blocks in cuts:
        heights = jax.random.uniform(jax.random.fold_in(jax.random.fold_in(key, 6), dim), (blocks,), jnp.float32, least / len(cuts), largest / len(cuts))
        factor_of = factor_of * jnp.repeat(jnp.exp(heights), extent[dim] // blocks).reshape((-1,) + (1,) * (len(extent) - 1 - dim))
    return factor_of


def deal_out(rng, own, number, rows, number_of, top, reach, slope):
    order = jax.random.permutation(rng, number_of)
    crowded, ordinary = load_shares(number_of, rows * top, reach, slope, True), load_shares(number_of, rows * top, reach, slope, False)
    places = jnp.arange(number_of)

    def named(sizes, offset_by):
        used = int((sizes > 0).sum())
        fixed = max(1, used // 4)
        moved = fixed + (places - fixed + offset_by * (used - fixed)) % max(1, number_of - fixed)
        return jnp.zeros((number_of,), jnp.int32).at[order[jnp.where(places < fixed, places, moved)]].set(jnp.asarray(sizes, jnp.int32))

    sizes = jnp.where(number % 4 == 0, named(crowded, number // 4), named(ordinary, number - number // 4 - 1))
    mixed = jax.random.permutation(jax.random.fold_in(own, 3), number_of)
    source_of, receiver = mixed[0:number_of // 2 * 2:2], mixed[1:number_of // 2 * 2:2]
    slack = jnp.minimum(sizes[source_of] - 1, reach - sizes[receiver]) // 2
    slack = jnp.where((source_of == order[0]) | (receiver == order[0]) | (sizes[receiver] == 0), 0, jnp.maximum(slack, 0))
    moved = jax.random.randint(jax.random.fold_in(own, 4), (number_of // 2,), 0, 1 << 20) % (slack + 1)
    sizes = sizes.at[source_of].add(-moved).at[receiver].add(moved)
    items = jnp.searchsorted(jnp.cumsum(sizes), jnp.arange(rows * top), side="right").astype(jnp.int32)
    table = items.reshape(top, rows).T
    table = table[jax.random.permutation(jax.random.fold_in(own, 1), rows)]
    offset_by = jax.random.randint(jax.random.fold_in(own, 2), (rows, 1), 0, top)
    return jnp.take_along_axis(table, (jnp.arange(top)[None, :] + offset_by) % top, axis=1)


def load_shares(count, total, bound, skew, full):
    loads = [(1 << 20) // math.isqrt(rank ** skew) + 1 for rank in range(1, count + 1)]
    largest = bound if full else min(bound, max(-(-total // count), total * loads[0] // sum(loads)))
    least = 1 if total - largest >= count - 1 else 0
    given, surplus = [largest] + [least] * (count - 1), total - largest - least * (count - 1)
    while surplus > 0:
        candidates = [i for i in range(1, count) if given[i] < largest] or [i for i in range(1, count) if given[i] < bound]
        mass, budget = sum([loads[i] for i in candidates]), surplus
        for i in candidates:
            addition = min(bound - given[i], max(1, budget * loads[i] // mass), surplus)
            given[i] = given[i] + addition
            surplus = surplus - addition
    return np.array(given)


def normal_values(key, extent, scale, limit, cuts=(), held_as=jnp.bfloat16):
    values = jax.random.normal(key, extent, jnp.float32) * scale
    if len(cuts) > 0:
        values = shard_levels(key, extent, cuts, -0.22, 0.18) * values
    return jnp.clip(values, min=-limit, max=limit).astype(held_as)


def setup_inputs(seed: int = 0) -> dict:
    key_of = jax.random.split(jax.random.key(seed), 15)
    queries = draw_queries(jax.random.fold_in(key_of[14], 71), 0)
    prefix_keys = draw_prefix_keys(jax.random.fold_in(key_of[14], 71), 0)
    prefix_values = normal_values(key_of[2], (REQUESTS, PREFIX, KVH * HD), 1.0, 6.0, ((0, 4), (1, 8)))
    suffix_keys = normal_values(key_of[3], (REQUESTS, R, KVH * HD), 8.0, 48.0, ((0, 4), (1, 8)))
    suffix_values = normal_values(key_of[4], (REQUESTS, R, KVH * HD), 1.0, 6.0, ((0, 4), (1, 8)))
    parents = draw_parents(jax.random.fold_in(key_of[14], 71), 0)
    out_proj = normal_values(key_of[6], (HEADS * HD, D), (HEADS * HD) ** -0.5, 0.09375, ((0, 8),))
    residual = normal_values(key_of[7], (REQUESTS, R, D), 1.0, 6.0, ((0, 4), (1, 8)))
    norm_gain = jnp.clip(1.0 + 0.1 * jax.random.normal(key_of[8], (D,), jnp.float32), 0.5, 1.5)
    router = normal_values(key_of[9], (D, EXPERTS), D ** -0.5, 0.09375)
    routes_keys = jax.random.split(jax.random.fold_in(key_of[10], 1), REQUESTS * R // ROWS_DEV)
    routes_turns = jax.random.permutation(jax.random.fold_in(key_of[10], 3), REQUESTS * R // ROWS_DEV)
    routes = jax.vmap(lambda own, number: deal_out(jax.random.fold_in(key_of[10], 2), own, number, ROWS_DEV, EXPERTS, TOP, CAP, 2))(routes_keys, routes_turns).reshape((REQUESTS, R, TOP))
    expert_gate = normal_values(key_of[11], (EXPERTS, D, EFF), D ** -0.5, 0.09375, ((0, 32),))
    expert_up = normal_values(key_of[12], (EXPERTS, D, EFF), D ** -0.5, 0.09375, ((0, 32),))
    expert_down = normal_values(key_of[13], (EXPERTS, EFF, D), EFF ** -0.5, 0.21875, ((0, 32),))
    return dict(queries=queries, prefix_keys=prefix_keys, prefix_values=prefix_values, suffix_keys=suffix_keys, suffix_values=suffix_values, parents=parents, out_proj=out_proj, residual=residual, norm_gain=norm_gain, router=router, routes=routes, expert_gate=expert_gate, expert_up=expert_up, expert_down=expert_down)


EPSILON = 1e-06

def visible_mask(parent_row):
    count = parent_row.shape[0]
    positions = jnp.arange(count, dtype=jnp.int32)
    current = positions
    visible = current[:, None] == positions[None, :]
    for level in range(DEPTH - 1):
        current = parent_row[current].astype(jnp.int32)
        visible = visible | (current[:, None] == positions[None, :])
    return visible

def request_attention(inputs):
    query_rows, key_rows, value_rows, suffix_key_rows, suffix_value_rows, parent_row = inputs
    visible = visible_mask(parent_row)
    group = HEADS // KVH
    scale = HD ** (-0.5)
    pieces = []
    for head_kv in range(KVH):
        query_block = query_rows[:, head_kv * group * HD:(head_kv + 1) * group * HD].reshape(R, group, HD).astype(jnp.float32)
        key_pre = key_rows[:, head_kv * HD:(head_kv + 1) * HD].astype(jnp.float32)
        value_pre = value_rows[:, head_kv * HD:(head_kv + 1) * HD].astype(jnp.float32)
        key_suf = suffix_key_rows[:, head_kv * HD:(head_kv + 1) * HD].astype(jnp.float32)
        value_suf = suffix_value_rows[:, head_kv * HD:(head_kv + 1) * HD].astype(jnp.float32)
        score_pre = jnp.einsum('rgd,kd->rgk', query_block, key_pre) * scale
        score_suf = jnp.einsum('rgd,jd->rgj', query_block, key_suf) * scale
        score_suf = jnp.where(visible[:, None, :], score_suf, -jnp.inf)
        top = jnp.maximum(lax.optimization_barrier(jnp.max(score_pre, axis=2)), lax.optimization_barrier(jnp.max(score_suf, axis=2)))
        weight_pre = jnp.exp(score_pre - top[:, :, None])
        weight_suf = jnp.exp(score_suf - top[:, :, None])
        total = lax.optimization_barrier(jnp.sum(weight_pre, axis=2)) + lax.optimization_barrier(jnp.sum(weight_suf, axis=2))
        rounded_pre = weight_pre.astype(jnp.bfloat16).astype(jnp.float32)
        rounded_suf = weight_suf.astype(jnp.bfloat16).astype(jnp.float32)
        summed = jnp.einsum('rgk,kd->rgd', rounded_pre, value_pre) + jnp.einsum('rgj,jd->rgd', rounded_suf, value_suf)
        pieces.append((summed / total[:, :, None]).astype(jnp.bfloat16).reshape(R, group * HD))
    return jnp.concatenate(pieces, axis=1)

def reference(queries, prefix_keys, prefix_values, suffix_keys, suffix_values, parents, out_proj, residual, norm_gain, router, routes, expert_gate, expert_up, expert_down):
    attention = lax.map(request_attention, (queries, prefix_keys, prefix_values, suffix_keys, suffix_values, parents))
    flat_attention = attention.reshape(REQUESTS * R, HEADS * HD)
    projected = jnp.dot(flat_attention, out_proj, preferred_element_type=jnp.float32)
    mixed = residual.reshape(REQUESTS * R, D).astype(jnp.float32) + projected
    inverse = lax.rsqrt(lax.optimization_barrier(jnp.mean(mixed * mixed, axis=1, keepdims=True)) + EPSILON)
    normed = (mixed * inverse * norm_gain[None, :]).astype(jnp.bfloat16)
    logits = jnp.dot(normed, router, preferred_element_type=jnp.float32)
    chosen_ids = routes.reshape(REQUESTS * R, TOP).astype(jnp.int32)
    chosen = jnp.take_along_axis(logits, chosen_ids, axis=1)
    sig = jax.nn.sigmoid(chosen)
    gates = sig / lax.optimization_barrier(jnp.sum(sig, axis=1, keepdims=True))
    flat_ids = chosen_ids.reshape(-1)
    assignments = flat_ids.shape[0]
    most_load = N_SEQ * N_GRP * CAP
    order = jnp.argsort(flat_ids, stable=True).astype(jnp.int32)
    counts = lax.optimization_barrier(jnp.sum((flat_ids[:, None] == jnp.arange(EXPERTS, dtype=jnp.int32)[None, :]).astype(jnp.int32), axis=0)).astype(jnp.int32)
    offsets = (jnp.cumsum(counts) - counts).astype(jnp.int32)
    order_padded = jnp.concatenate([order, jnp.zeros((most_load,), jnp.int32)])

    def one_expert(inputs):
        offset, count, gate_w, up_w, down_w = inputs
        index = lax.dynamic_slice(order_padded, (offset.astype(jnp.int32),), (most_load,))
        valid = jnp.arange(most_load, dtype=jnp.int32) < count
        rows = normed[index // TOP]
        gate_part = jnp.dot(rows, gate_w, preferred_element_type=jnp.float32)
        up_part = jnp.dot(rows, up_w, preferred_element_type=jnp.float32)
        act = (jax.nn.silu(gate_part) * up_part).astype(jnp.bfloat16)
        result = jnp.dot(act, down_w, preferred_element_type=jnp.float32).astype(jnp.bfloat16)
        return (index, jnp.where(valid[:, None], result, jnp.zeros_like(result)))
    indices, results = lax.map(one_expert, (offsets, counts, expert_gate, expert_up, expert_down))
    placed = jnp.zeros((assignments, D), jnp.float32).at[indices.reshape(-1)].add(results.reshape(-1, D).astype(jnp.float32))
    moe = lax.optimization_barrier(jnp.sum(placed.reshape(REQUESTS * R, TOP, D) * gates[:, :, None], axis=1))
    return (mixed + moe).astype(jnp.bfloat16).reshape(REQUESTS, R, D)
```

```python
import functools
import math

import jax
import jax.numpy as jnp
from jax import lax
from jax.experimental import pallas as pl
from jax.experimental.pallas import tpu as pltpu
from jax.sharding import PartitionSpec as P

HEADS = 32
KVH = 4
HD = 128
DEPTH = 8
EPSILON = 1e-06
MESH = pl.DeviceIdType.MESH
SCALE = HD ** (-0.5) * math.log2(math.e)
F32 = jnp.float32
BF16 = jnp.bfloat16
VLIMIT = 60 * 1024 * 1024
SEMS = 96


class Place:
    def __init__(self, n_seq, n_grp):
        self.nx = 2 ** (int(math.log2(n_seq)) // 2)
        self.nz = n_seq // self.nx
        self.ny = n_grp // 2
        s, g = lax.axis_index("seq"), lax.axis_index("grp")
        self.z, self.x = s // self.nx, lax.rem(s, self.nx)
        self.y, self.c = g // 2, lax.rem(g, 2)

    def device(self, z=None, x=None, y=None, c=None):
        z = self.z if z is None else z
        x = self.x if x is None else x
        y = self.y if y is None else y
        c = self.c if c is None else c
        return (z * self.nx + x, y * 2 + c)

    def zk(self, k):
        return lax.rem(self.z + k + self.nz, self.nz)

    def xk(self, k):
        return lax.rem(self.x + k + self.nx, self.nx)

    def yk(self, k):
        return lax.rem(self.y + k + self.ny, self.ny)


def dims(n_seq, n_grp):
    nx = 2 ** (int(math.log2(n_seq)) // 2)
    return n_seq // nx, nx, n_grp // 2


def greet(peers):
    barrier = pltpu.get_barrier_semaphore()
    for peer in peers:
        pl.semaphore_signal(barrier, inc=1, device_id=peer, device_id_type=MESH)
    pl.semaphore_wait(barrier, len(peers))


class Copies:
    def __init__(self, send_sems, recv_sems):
        self.send_sems, self.recv_sems, self.started = send_sems, recv_sems, []

    def start(self, src, dst, device):
        n = len(self.started)
        copy = pltpu.make_async_remote_copy(
            src_ref=src,
            dst_ref=dst,
            send_sem=self.send_sems.at[n],
            recv_sem=self.recv_sems.at[n],
            device_id=device,
            device_id_type=MESH,
        )
        copy.start()
        self.started.append(copy)
        return copy

    def finish(self):
        for copy in self.started:
            copy.wait_send()


def axis_peers(p, grp=True):
    peers = [p.device(z=p.zk(k)) for k in range(1, p.nz)]
    peers += [p.device(x=p.xk(k)) for k in range(1, p.nx)]
    if grp:
        peers += [p.device(y=p.yk(k)) for k in range(1, p.ny)]
        peers += [p.device(c=1 - p.c)]
    return peers


def call(kernel, outs, ins, scratch, ident):
    vmem = pl.BlockSpec(memory_space=pltpu.VMEM)
    return pl.pallas_call(
        kernel,
        out_shape=outs,
        in_specs=[vmem] * len(ins),
        out_specs=jax.tree.map(lambda _: vmem, outs),
        scratch_shapes=list(scratch)
        + [pltpu.SemaphoreType.DMA((SEMS,)), pltpu.SemaphoreType.DMA((SEMS,))],
        compiler_params=pltpu.CompilerParams(
            collective_id=ident, has_side_effects=True, vmem_limit_bytes=VLIMIT
        ),
    )(*ins)


def gather_kernel(n_seq, n_grp, in_ref, out_ref, send_sems, recv_sems):
    p = Place(n_seq, n_grp)
    greet(axis_peers(p, grp=False))
    copies = Copies(send_sems, recv_sems)
    z_copies = [
        copies.start(in_ref, out_ref.at[p.z, p.x], p.device(z=p.zk(k))) for k in range(1, p.nz)
    ]
    x_copies = [
        copies.start(in_ref, out_ref.at[p.z, p.x], p.device(x=p.xk(j))) for j in range(1, p.nx)
    ]
    out_ref[p.z, p.x] = in_ref[...]
    for k in range(1, p.nz):
        z_copies[k - 1].wait_recv()
        block = out_ref.at[p.zk(-k), p.x]
        x_copies += [copies.start(block, block, p.device(x=p.xk(j))) for j in range(1, p.nx)]
    for copy in x_copies:
        copy.wait_recv()
    copies.finish()


def prefix_kernel(group, q_ref, k_ref, v_ref, o_ref, m_ref, l_ref):
    key, value = k_ref[...], v_ref[...]
    for h in range(group):
        s = lax.dot_general(
            key, q_ref[:, h * HD : (h + 1) * HD], (((1,), (1,)), ((), ())),
            preferred_element_type=F32,
        ) * SCALE
        m = jnp.max(s, axis=0, keepdims=True)
        w = jnp.exp2(s - m)
        l_ref[h : h + 1, :] = jnp.sum(w, axis=0, keepdims=True)
        m_ref[h : h + 1, :] = m
        o_ref[h * HD : (h + 1) * HD, :] = lax.dot_general(
            value, w.astype(BF16), (((0,), (0,)), ((), ())), preferred_element_type=F32
        )


def merge_kernel(
    n_seq, n_grp, o_ref, m_ref, l_ref, out_ref, total_ref, max_ref,
    m_buf, l_buf, s_buf, x_buf, a_buf, z_buf, send_sems, recv_sems,
):
    p = Place(n_seq, n_grp)
    s, g = lax.axis_index("seq"), lax.axis_index("grp")
    own_heads = m_ref.shape[1]
    others = [lax.rem(s + j, n_seq) for j in range(1, n_seq)]
    greet([(other, g) for other in others])
    copies = Copies(send_sems, recv_sems)
    small = []
    for j, other in enumerate(others):
        small.append(copies.start(m_ref, m_buf.at[j], (other, g)))
    for j, other in enumerate(others):
        small.append(copies.start(l_ref.at[other], l_buf.at[j], (other, g)))
    for copy in small[: n_seq - 1]:
        copy.wait_recv()
    whole = m_ref[...]
    for j in range(n_seq - 1):
        whole = jnp.maximum(whole, m_buf[j])
    x_buf_copies = []
    m_buf[n_seq - 1] = whole
    order = list(range(1, p.nz)) + [0]
    for k in order:
        row = []
        for j in list(range(1, p.nx)) + [0]:
            t = p.zk(k) * p.nx + p.xk(j)
            factor = jnp.exp2(m_ref[t] - m_buf[n_seq - 1, t])
            for h in range(own_heads):
                s_buf[t, h * HD : (h + 1) * HD, :] = (
                    o_ref[t, h * HD : (h + 1) * HD, :] * factor[h : h + 1, :]
                ).astype(BF16)
            if j:
                row.append(
                    copies.start(s_buf.at[t], x_buf.at[j - 1, k], p.device(x=p.xk(j)))
                )
        x_buf_copies.append(row)
    z_copies = []
    last = None
    for k, row in zip(order, x_buf_copies):
        t = p.zk(k) * p.nx + p.x
        acc = s_buf[t].astype(F32)
        for j, copy in enumerate(row):
            copy.wait_recv()
            acc = acc + x_buf[j, k].astype(F32)
        if k:
            a_buf[k - 1] = acc.astype(BF16)
            z_copies.append(copies.start(a_buf.at[k - 1], z_buf.at[k - 1], p.device(z=p.zk(k))))
        else:
            last = acc
    out_ref[...] = last
    for copy in small[n_seq - 1 :]:
        copy.wait_recv()
    own_max = m_buf[n_seq - 1, s]
    total = l_ref[s] * jnp.exp2(m_ref[s] - own_max)
    for j in range(n_seq - 1):
        total = total + l_buf[j] * jnp.exp2(m_buf[j, s] - own_max)
    total_ref[...] = total
    max_ref[...] = own_max
    for k in range(1, p.nz):
        z_copies[k - 1].wait_recv()
        out_ref[...] += z_buf[k - 1].astype(F32)
    copies.finish()


def project_kernel(own_heads, q_ref, k_ref, v_ref, par_ref, o_ref, l_ref, m_ref, w_ref, out_ref, att_ref):
    rows = q_ref.shape[0]

    @pl.when(pl.program_id(0) == 0)
    def _():
        j_index = lax.broadcasted_iota(jnp.int32, (rows, rows), 0)
        i_index = lax.broadcasted_iota(jnp.int32, (rows, rows), 1)
        step = (par_ref[...] == j_index).astype(F32) + (i_index == j_index).astype(F32)
        paths, power = step, step
        for _ in range(int(math.log2(DEPTH)) - 1):
            power = jnp.dot(power.astype(BF16), power.astype(BF16), preferred_element_type=F32)
            paths = jnp.dot(paths.astype(BF16), power.astype(BF16), preferred_element_type=F32)
        seen = paths > 0.5
        for h in range(own_heads):
            s = lax.dot_general(
                k_ref[...], q_ref[:, h * HD : (h + 1) * HD], (((1,), (1,)), ((), ())),
                preferred_element_type=F32,
            ) * SCALE
            s = jnp.where(seen, s, -jnp.inf)
            before = m_ref[h : h + 1, :]
            top = jnp.maximum(before, jnp.max(s, axis=0, keepdims=True))
            w = jnp.exp2(s - top)
            scale = jnp.exp2(before - top)
            total = l_ref[h : h + 1, :] * scale + jnp.sum(w, axis=0, keepdims=True)
            o = lax.dot_general(
                v_ref[...], w.astype(BF16), (((0,), (0,)), ((), ())), preferred_element_type=F32
            )
            o = (o_ref[h * HD : (h + 1) * HD, :] * scale + o) / total
            att_ref[:, h * HD : (h + 1) * HD] = o.T.astype(BF16)

    out_ref[...] = jnp.dot(att_ref[...], w_ref[...], preferred_element_type=F32).astype(BF16)


def norm_kernel(
    n_seq, n_grp, experts, proj_ref, res_ref, gain_ref, router_ref, chosen_ref,
    mixed_ref, out_ref, x_buf, a_buf, z_buf, send_sems, recv_sems,
):
    p = Place(n_seq, n_grp)
    greet(axis_peers(p))
    copies = Copies(send_sems, recv_sems)
    order = list(range(1, p.nz)) + [0]
    x_copies = [
        [
            copies.start(proj_ref.at[p.zk(k), p.xk(j)], x_buf.at[j - 1, k], p.device(x=p.xk(j)))
            for j in range(1, p.nx)
        ]
        for k in order
    ]
    z_copies = []
    mixed = None
    for k, row in zip(order, x_copies):
        acc = proj_ref[p.zk(k), p.x].astype(F32)
        for j, copy in enumerate(row):
            copy.wait_recv()
            acc = acc + x_buf[j, k].astype(F32)
        if k:
            a_buf[k - 1] = acc.astype(BF16)
            z_copies.append(copies.start(a_buf.at[k - 1], z_buf.at[k - 1], p.device(z=p.zk(k))))
        else:
            mixed_ref[...] = acc + res_ref[...].astype(F32)
    for k in range(1, p.nz):
        z_copies[k - 1].wait_recv()
        mixed_ref[...] += z_buf[k - 1].astype(F32)
    mixed = mixed_ref[...]
    inverse = lax.rsqrt(jnp.mean(mixed * mixed, axis=1, keepdims=True) + EPSILON)
    normed = (mixed * inverse * gain_ref[...]).astype(BF16)
    width = normed.shape[1]
    own = out_ref.at[p.c, p.z, p.x, p.y]
    own[:, :width] = normed
    logits = jnp.dot(normed, router_ref[...], preferred_element_type=F32)
    sig = jax.nn.sigmoid(logits) * chosen_ref[...]
    lane = lax.broadcasted_iota(jnp.int32, sig.shape, 1)
    gates = sig / jnp.sum(jnp.where(lane < experts, sig, 0.0), axis=1, keepdims=True)
    high = gates.astype(BF16).astype(F32)
    own[:, width:] = jnp.where(lane < experts, high, gates - high).astype(BF16)

    half = width // 2
    cuts = (pl.ds(0, half), pl.ds(half, out_ref.shape[5] - half))
    a, b = cuts
    c = p.c
    z_copies = []
    for k in range(1, p.nz):
        z_copies.append(
            [
                copies.start(
                    out_ref.at[c, p.z, p.x, p.y, :, cut], out_ref.at[c, p.z, p.x, p.y, :, cut],
                    p.device(z=p.zk(k)),
                )
                for cut in cuts
            ]
        )
    first, second, core = [], [], []
    ks = list(range(p.nz))

    def spread(k):
        block = (c, p.zk(-k), p.x, p.y, slice(None))
        row = []
        for j in range(1, p.nx):
            ref = out_ref.at[block + (a,)]
            row.append(copies.start(ref, ref, p.device(x=p.xk(j))))
        for j in range(1, p.ny):
            ref = out_ref.at[block + (b,)]
            row.append(copies.start(ref, ref, p.device(y=p.yk(j))))
        return row

    def widen(k, row):
        for copy in row:
            copy.wait_recv()
        done = []
        for j in range(1, p.ny):
            ref = out_ref.at[c, p.zk(-k), :, p.y, :, a]
            done.append(copies.start(ref, ref, p.device(y=p.yk(j))))
        for j in range(1, p.nx):
            ref = out_ref.at[c, p.zk(-k), p.x, :, :, b]
            done.append(copies.start(ref, ref, p.device(x=p.xk(j))))
        return done

    def share(k, row):
        for copy in row:
            copy.wait_recv()
        ref = out_ref.at[c, p.zk(-k)]
        return copies.start(ref, ref, p.device(c=1 - c))

    for k in ks:
        if k:
            for copy in z_copies[k - 1]:
                copy.wait_recv()
        first.append(spread(k))
        if k >= 1:
            second.append(widen(k - 1, first[k - 1]))
        if k >= 2:
            core.append(share(k - 2, second[k - 2]))
    second.append(widen(ks[-1], first[-1]))
    core.append(share(ks[-2], second[-2]))
    core.append(share(ks[-1], second[-1]))
    for copy in core:
        copy.wait_recv()
    copies.finish()


def combine_kernel(
    n_seq, n_grp, in_ref, mixed_ref, out_ref,
    c_buf, acc, a1, b1, a2, b2, a3, b3, a4, b4, a5, b5, send_sems, recv_sems,
):
    p = Place(n_seq, n_grp)
    greet(axis_peers(p))
    copies = Copies(send_sems, recv_sems)
    width = out_ref.shape[1]
    half = width // 2
    a, b = pl.ds(0, half), pl.ds(half, width - half)
    order = list(range(1, p.nz)) + [0]
    core = [
        copies.start(in_ref.at[1 - p.c, p.zk(k)], c_buf.at[k], p.device(c=1 - p.c)) for k in order
    ]
    first, second, third = [], [], []

    def core_sum(i):
        k = order[i]
        core[i].wait_recv()
        for x in range(p.nx):
            for y in range(p.ny):
                acc[k, x, y] = (
                    in_ref[p.c, p.zk(k), x, y].astype(F32) + c_buf[k, x, y].astype(F32)
                ).astype(BF16)
        row = []
        for j in range(1, p.ny):
            row.append(
                copies.start(acc.at[k, :, p.yk(j), :, a], a1.at[j - 1, k], p.device(y=p.yk(j)))
            )
        for j in range(1, p.nx):
            row.append(
                copies.start(acc.at[k, p.xk(j), :, :, b], b1.at[j - 1, k], p.device(x=p.xk(j)))
            )
        first.append(row)

    def first_sum(i):
        k = order[i]
        for copy in first[i]:
            copy.wait_recv()
        for x in range(p.nx):
            total = acc[k, x, p.y, :, a].astype(F32)
            for j in range(p.ny - 1):
                total = total + a1[j, k, x].astype(F32)
            a2[k, x] = total.astype(BF16)
        for y in range(p.ny):
            total = acc[k, p.x, y, :, b].astype(F32)
            for j in range(p.nx - 1):
                total = total + b1[j, k, y].astype(F32)
            b2[k, y] = total.astype(BF16)
        row = []
        for j in range(1, p.nx):
            row.append(copies.start(a2.at[k, p.xk(j)], a3.at[j - 1, k], p.device(x=p.xk(j))))
        for j in range(1, p.ny):
            row.append(copies.start(b2.at[k, p.yk(j)], b3.at[j - 1, k], p.device(y=p.yk(j))))
        second.append(row)

    def second_sum(i):
        k = order[i]
        for copy in second[i]:
            copy.wait_recv()
        left = a2[k, p.x].astype(F32)
        for j in range(p.nx - 1):
            left = left + a3[j, k].astype(F32)
        right = b2[k, p.y].astype(F32)
        for j in range(p.ny - 1):
            right = right + b3[j, k].astype(F32)
        if k:
            a4[k - 1] = left.astype(BF16)
            b4[k - 1] = right.astype(BF16)
            third.append(copies.start(a4.at[k - 1], a5.at[k - 1], p.device(z=p.zk(k))))
            third.append(copies.start(b4.at[k - 1], b5.at[k - 1], p.device(z=p.zk(k))))
            return None
        return left, right

    n = len(order)
    for i in range(n):
        core_sum(i)
        if i >= 1:
            first_sum(i - 1)
        if i >= 2:
            second_sum(i - 2)
    first_sum(n - 1)
    second_sum(n - 2)
    left, right = second_sum(n - 1)
    left = left + mixed_ref[:, a]
    right = right + mixed_ref[:, b]
    for copy in third:
        copy.wait_recv()
    for k in range(p.nz - 1):
        left = left + a5[k].astype(F32)
        right = right + b5[k].astype(F32)
    out_ref[:, a] = left.astype(BF16)
    out_ref[:, b] = right.astype(BF16)
    copies.finish()


def local(
    queries, prefix_keys, prefix_values, suffix_keys, suffix_values, parents, out_proj,
    residual, norm_gain, router, routes, expert_gate, expert_up, expert_down,
):
    n_seq, n_grp = lax.axis_size("seq"), lax.axis_size("grp")
    nz, nx, ny = dims(n_seq, n_grp)
    s, g = lax.axis_index("seq"), lax.axis_index("grp")
    rows, width = queries.shape[1], queries.shape[2]
    total_rows = rows * n_seq
    keys = prefix_keys.shape[1]
    kv_width = suffix_keys.shape[2]
    group = HEADS // KVH
    own_heads = HEADS // n_seq
    own_width = own_heads * HD
    vmem = pltpu.VMEM

    packed = jnp.concatenate([queries[0], suffix_keys[0], suffix_values[0]], axis=1)
    pack_width = packed.shape[1]
    gathered = call(
        functools.partial(gather_kernel, n_seq, n_grp),
        jax.ShapeDtypeStruct((nz, nx, rows, pack_width), BF16),
        [packed], [], 0,
    ).reshape(total_rows, pack_width)

    o, m, l = pl.pallas_call(
        functools.partial(prefix_kernel, group),
        grid=(KVH,),
        in_specs=[
            pl.BlockSpec((total_rows, group * HD), lambda i: (0, i)),
            pl.BlockSpec((keys, HD), lambda i: (0, i)),
            pl.BlockSpec((keys, HD), lambda i: (0, i)),
        ],
        out_specs=[
            pl.BlockSpec((group * HD, total_rows), lambda i: (i, 0)),
            pl.BlockSpec((group, total_rows), lambda i: (i, 0)),
            pl.BlockSpec((group, total_rows), lambda i: (i, 0)),
        ],
        out_shape=[
            jax.ShapeDtypeStruct((HEADS * HD, total_rows), F32),
            jax.ShapeDtypeStruct((HEADS, total_rows), F32),
            jax.ShapeDtypeStruct((HEADS, total_rows), F32),
        ],
        compiler_params=pltpu.CompilerParams(vmem_limit_bytes=VLIMIT),
    )(gathered, prefix_keys[0], prefix_values[0])

    o_own, l_own, m_own = call(
        functools.partial(merge_kernel, n_seq, n_grp),
        [
            jax.ShapeDtypeStruct((own_width, total_rows), F32),
            jax.ShapeDtypeStruct((own_heads, total_rows), F32),
            jax.ShapeDtypeStruct((own_heads, total_rows), F32),
        ],
        [
            o.reshape(n_seq, own_width, total_rows),
            m.reshape(n_seq, own_heads, total_rows),
            l.reshape(n_seq, own_heads, total_rows),
        ],
        [
            vmem((n_seq, n_seq, own_heads, total_rows), F32),
            vmem((n_seq - 1, own_heads, total_rows), F32),
            vmem((n_seq, own_width, total_rows), BF16),
            vmem((nx - 1, nz, own_width, total_rows), BF16),
            vmem((nz - 1, own_width, total_rows), BF16),
            vmem((nz - 1, own_width, total_rows), BF16),
        ],
        1,
    )

    kv_index = s * own_heads // group
    own_q = lax.dynamic_slice_in_dim(gathered, s * own_width, own_width, 1)
    own_k = lax.dynamic_slice_in_dim(gathered, width + kv_index * HD, HD, 1)
    own_v = lax.dynamic_slice_in_dim(gathered, width + kv_width + kv_index * HD, HD, 1)
    tile = min(1024, width)
    whole = lambda *shape: pl.BlockSpec(shape, lambda i: (0,) * len(shape))
    projected = pl.pallas_call(
        functools.partial(project_kernel, own_heads),
        grid=(width // tile,),
        in_specs=[
            whole(total_rows, own_width), whole(total_rows, HD), whole(total_rows, HD),
            whole(1, total_rows), whole(own_width, total_rows), whole(own_heads, total_rows),
            whole(own_heads, total_rows), pl.BlockSpec((own_width, tile), lambda i: (0, i)),
        ],
        out_specs=pl.BlockSpec((total_rows, tile), lambda i: (0, i)),
        out_shape=jax.ShapeDtypeStruct((total_rows, width), BF16),
        scratch_shapes=[vmem((total_rows, own_width), BF16)],
        compiler_params=pltpu.CompilerParams(vmem_limit_bytes=VLIMIT),
    )(own_q, own_k, own_v, parents, o_own, l_own, m_own, out_proj)

    experts = router.shape[1]
    lanes = -(-2 * experts // 128) * 128
    chosen = jnp.sum(
        (routes[0][:, :, None] == jnp.arange(experts, dtype=jnp.int32)).astype(F32), axis=1
    )
    pad = ((0, 0), (0, lanes - 2 * experts))
    chosen = jnp.pad(jnp.concatenate([chosen, chosen], axis=1), pad)
    router_wide = jnp.pad(jnp.concatenate([router, router], axis=1), pad)
    mixed, arrived = call(
        functools.partial(norm_kernel, n_seq, n_grp, experts),
        [
            jax.ShapeDtypeStruct((rows, width), F32),
            jax.ShapeDtypeStruct((2, nz, nx, ny, rows, width + lanes), BF16),
        ],
        [
            projected.reshape(nz, nx, rows, width), residual[0], norm_gain[None], router_wide,
            chosen,
        ],
        [
            vmem((nx - 1, nz, rows, width), BF16),
            vmem((nz - 1, rows, width), BF16),
            vmem((nz - 1, rows, width), BF16),
        ],
        2,
    )

    flat = arrived.reshape(-1, width + lanes)
    x = flat[:, :width]
    parts = flat[:, width:].astype(F32)
    expert = s * n_grp + g
    lane = jnp.arange(lanes, dtype=jnp.int32)
    mine = (lane == expert) | (lane == expert + experts)
    gate = jnp.sum(jnp.where(mine[None, :], parts, 0.0), axis=1, keepdims=True)
    gate_part = jnp.dot(x, expert_gate[0], preferred_element_type=F32)
    up_part = jnp.dot(x, expert_up[0], preferred_element_type=F32)
    act = (jax.nn.silu(gate_part) * up_part).astype(BF16)
    result = jnp.dot(act, expert_down[0], preferred_element_type=F32).astype(BF16)
    weighted = (result.astype(F32) * gate).astype(BF16)

    half = width // 2
    out = call(
        functools.partial(combine_kernel, n_seq, n_grp),
        jax.ShapeDtypeStruct((rows, width), BF16),
        [weighted.reshape(2, nz, nx, ny, rows, width), mixed],
        [
            vmem((nz, nx, ny, rows, width), BF16),
            vmem((nz, nx, ny, rows, width), BF16),
            vmem((ny - 1, nz, nx, rows, half), BF16),
            vmem((nx - 1, nz, ny, rows, half), BF16),
            vmem((nz, nx, rows, half), BF16),
            vmem((nz, ny, rows, half), BF16),
            vmem((nx - 1, nz, rows, half), BF16),
            vmem((ny - 1, nz, rows, half), BF16),
            vmem((nz - 1, rows, half), BF16),
            vmem((nz - 1, rows, half), BF16),
            vmem((nz - 1, rows, half), BF16),
            vmem((nz - 1, rows, half), BF16),
        ],
        3,
    )
    return out[None]


def solution(mesh):
    in_specs = (
        P("grp", "seq", None),
        P("grp", "seq", None),
        P("grp", "seq", None),
        P("grp", "seq", None),
        P("grp", "seq", None),
        P("grp", None),
        P("seq", None),
        P("grp", "seq", None),
        P(),
        P(),
        P("grp", "seq", None),
        P(("seq", "grp"), None, None),
        P(("seq", "grp"), None, None),
        P(("seq", "grp"), None, None),
    )
    out_specs = P("grp", "seq", None)
    return jax.shard_map(local, mesh=mesh, in_specs=in_specs, out_specs=out_specs, check_vma=False)
```

```python
import functools
import math

import jax
import jax.numpy as jnp
from jax import lax
from jax.experimental import pallas as pl
from jax.experimental.pallas import tpu as pltpu
from jax.sharding import PartitionSpec as P

HEADS = 32
KVH = 4
HD = 128
DEPTH = 8
EPSILON = 1e-06
MESH = pl.DeviceIdType.MESH
SCALE = HD ** (-0.5) * math.log2(math.e)
F32 = jnp.float32
BF16 = jnp.bfloat16
VLIMIT = 60 * 1024 * 1024
SEMS = 96


class Place:
    def __init__(self, n_seq, n_grp):
        self.nx = 2 ** (int(math.log2(n_seq)) // 2)
        self.nz = n_seq // self.nx
        self.ny = n_grp // 2
        s, g = lax.axis_index("seq"), lax.axis_index("grp")
        self.z, self.x = s // self.nx, lax.rem(s, self.nx)
        self.y, self.c = g // 2, lax.rem(g, 2)

    def device(self, z=None, x=None, y=None, c=None):
        z = self.z if z is None else z
        x = self.x if x is None else x
        y = self.y if y is None else y
        c = self.c if c is None else c
        return (z * self.nx + x, y * 2 + c)

    def zk(self, k):
        return lax.rem(self.z + k + self.nz, self.nz)

    def xk(self, k):
        return lax.rem(self.x + k + self.nx, self.nx)

    def yk(self, k):
        return lax.rem(self.y + k + self.ny, self.ny)


def dims(n_seq, n_grp):
    nx = 2 ** (int(math.log2(n_seq)) // 2)
    return n_seq // nx, nx, n_grp // 2


def greet(peers):
    barrier = pltpu.get_barrier_semaphore()
    for peer in peers:
        pl.semaphore_signal(barrier, inc=1, device_id=peer, device_id_type=MESH)
    pl.semaphore_wait(barrier, len(peers))


class Copies:
    def __init__(self, send_sems, recv_sems):
        self.send_sems, self.recv_sems, self.started = send_sems, recv_sems, []

    def start(self, src, dst, device):
        n = len(self.started)
        copy = pltpu.make_async_remote_copy(
            src_ref=src,
            dst_ref=dst,
            send_sem=self.send_sems.at[n],
            recv_sem=self.recv_sems.at[n],
            device_id=device,
            device_id_type=MESH,
        )
        copy.start()
        self.started.append(copy)
        return copy

    def finish(self):
        for copy in self.started:
            copy.wait_send()


def axis_peers(p, grp=True):
    peers = [p.device(z=p.zk(k)) for k in range(1, p.nz)]
    peers += [p.device(x=p.xk(k)) for k in range(1, p.nx)]
    if grp:
        peers += [p.device(y=p.yk(k)) for k in range(1, p.ny)]
        peers += [p.device(c=1 - p.c)]
    return peers


def call(kernel, outs, ins, scratch, ident):
    vmem = pl.BlockSpec(memory_space=pltpu.VMEM)
    return pl.pallas_call(
        kernel,
        out_shape=outs,
        in_specs=[vmem] * len(ins),
        out_specs=jax.tree.map(lambda _: vmem, outs),
        scratch_shapes=list(scratch)
        + [pltpu.SemaphoreType.DMA((SEMS,)), pltpu.SemaphoreType.DMA((SEMS,))],
        compiler_params=pltpu.CompilerParams(
            collective_id=ident, has_side_effects=True, vmem_limit_bytes=VLIMIT
        ),
    )(*ins)


def gather_kernel(n_seq, n_grp, in_ref, out_ref, send_sems, recv_sems):
    p = Place(n_seq, n_grp)
    greet(axis_peers(p, grp=False))
    copies = Copies(send_sems, recv_sems)
    z_copies = [
        copies.start(in_ref, out_ref.at[p.z, p.x], p.device(z=p.zk(k))) for k in range(1, p.nz)
    ]
    x_copies = [
        copies.start(in_ref, out_ref.at[p.z, p.x], p.device(x=p.xk(j))) for j in range(1, p.nx)
    ]
    out_ref[p.z, p.x] = in_ref[...]
    for k in range(1, p.nz):
        z_copies[k - 1].wait_recv()
        block = out_ref.at[p.zk(-k), p.x]
        x_copies += [copies.start(block, block, p.device(x=p.xk(j))) for j in range(1, p.nx)]
    for copy in x_copies:
        copy.wait_recv()
    copies.finish()


def prefix_kernel(group, q_ref, k_ref, v_ref, o_ref, m_ref, l_ref):
    key, value = k_ref[...], v_ref[...]
    for h in range(group):
        s = lax.dot_general(
            key, q_ref[:, h * HD : (h + 1) * HD], (((1,), (1,)), ((), ())),
            preferred_element_type=F32,
        ) * SCALE
        m = jnp.max(s, axis=0, keepdims=True)
        w = jnp.exp2(s - m)
        l_ref[h : h + 1, :] = jnp.sum(w, axis=0, keepdims=True)
        m_ref[h : h + 1, :] = m
        o_ref[h * HD : (h + 1) * HD, :] = lax.dot_general(
            value, w.astype(BF16), (((0,), (0,)), ((), ())), preferred_element_type=F32
        )


def merge_kernel(
    n_seq, n_grp, o_ref, m_ref, l_ref, out_ref, total_ref, max_ref,
    m_buf, l_buf, s_buf, x_buf, a_buf, z_buf, send_sems, recv_sems,
):
    p = Place(n_seq, n_grp)
    s, g = lax.axis_index("seq"), lax.axis_index("grp")
    own_heads = m_ref.shape[1]
    others = [lax.rem(s + j, n_seq) for j in range(1, n_seq)]
    greet([(other, g) for other in others])
    copies = Copies(send_sems, recv_sems)
    small = []
    for j, other in enumerate(others):
        small.append(copies.start(m_ref, m_buf.at[j], (other, g)))
    for j, other in enumerate(others):
        small.append(copies.start(l_ref.at[other], l_buf.at[j], (other, g)))
    for copy in small[: n_seq - 1]:
        copy.wait_recv()
    whole = m_ref[...]
    for j in range(n_seq - 1):
        whole = jnp.maximum(whole, m_buf[j])
    x_buf_copies = []
    m_buf[n_seq - 1] = whole
    order = list(range(1, p.nz)) + [0]
    for k in order:
        row = []
        for j in list(range(1, p.nx)) + [0]:
            t = p.zk(k) * p.nx + p.xk(j)
            factor = jnp.exp2(m_ref[t] - m_buf[n_seq - 1, t])
            for h in range(own_heads):
                s_buf[t, h * HD : (h + 1) * HD, :] = (
                    o_ref[t, h * HD : (h + 1) * HD, :] * factor[h : h + 1, :]
                ).astype(BF16)
            if j:
                row.append(
                    copies.start(s_buf.at[t], x_buf.at[j - 1, k], p.device(x=p.xk(j)))
                )
        x_buf_copies.append(row)
    z_copies = []
    last = None
    for k, row in zip(order, x_buf_copies):
        t = p.zk(k) * p.nx + p.x
        acc = s_buf[t].astype(F32)
        for j, copy in enumerate(row):
            copy.wait_recv()
            acc = acc + x_buf[j, k].astype(F32)
        if k:
            a_buf[k - 1] = acc.astype(BF16)
            z_copies.append(copies.start(a_buf.at[k - 1], z_buf.at[k - 1], p.device(z=p.zk(k))))
        else:
            last = acc
    out_ref[...] = last
    for copy in small[n_seq - 1 :]:
        copy.wait_recv()
    own_max = m_buf[n_seq - 1, s]
    total = l_ref[s] * jnp.exp2(m_ref[s] - own_max)
    for j in range(n_seq - 1):
        total = total + l_buf[j] * jnp.exp2(m_buf[j, s] - own_max)
    total_ref[...] = total
    max_ref[...] = own_max
    for k in range(1, p.nz):
        z_copies[k - 1].wait_recv()
        out_ref[...] += z_buf[k - 1].astype(F32)
    copies.finish()


def project_kernel(own_heads, q_ref, k_ref, v_ref, par_ref, o_ref, l_ref, m_ref, w_ref, out_ref, att_ref):
    rows = q_ref.shape[0]

    @pl.when(pl.program_id(0) == 0)
    def _():
        j_index = lax.broadcasted_iota(jnp.int32, (rows, rows), 0)
        i_index = lax.broadcasted_iota(jnp.int32, (rows, rows), 1)
        step = (par_ref[...] == j_index).astype(F32) + (i_index == j_index).astype(F32)
        paths, power = step, step
        for _ in range(int(math.log2(DEPTH)) - 1):
            power = jnp.dot(power.astype(BF16), power.astype(BF16), preferred_element_type=F32)
            paths = jnp.dot(paths.astype(BF16), power.astype(BF16), preferred_element_type=F32)
        seen = paths > 0.5
        for h in range(own_heads):
            s = lax.dot_general(
                k_ref[...], q_ref[:, h * HD : (h + 1) * HD], (((1,), (1,)), ((), ())),
                preferred_element_type=F32,
            ) * SCALE
            s = jnp.where(seen, s, -jnp.inf)
            before = m_ref[h : h + 1, :]
            top = jnp.maximum(before, jnp.max(s, axis=0, keepdims=True))
            w = jnp.exp2(s - top)
            scale = jnp.exp2(before - top)
            total = l_ref[h : h + 1, :] * scale + jnp.sum(w, axis=0, keepdims=True)
            o = lax.dot_general(
                v_ref[...], w.astype(BF16), (((0,), (0,)), ((), ())), preferred_element_type=F32
            )
            o = (o_ref[h * HD : (h + 1) * HD, :] * scale + o) / total
            att_ref[:, h * HD : (h + 1) * HD] = o.T.astype(BF16)

    out_ref[...] = jnp.dot(att_ref[...], w_ref[...], preferred_element_type=F32).astype(BF16)


def norm_kernel(
    n_seq, n_grp, experts, proj_ref, res_ref, gain_ref, router_ref, chosen_ref,
    mixed_ref, out_ref, x_buf, a_buf, z_buf, send_sems, recv_sems,
):
    p = Place(n_seq, n_grp)
    greet(axis_peers(p))
    copies = Copies(send_sems, recv_sems)
    order = list(range(1, p.nz)) + [0]
    x_copies = [
        [
            copies.start(proj_ref.at[p.zk(k), p.xk(j)], x_buf.at[j - 1, k], p.device(x=p.xk(j)))
            for j in range(1, p.nx)
        ]
        for k in order
    ]
    z_copies = []
    mixed = None
    for k, row in zip(order, x_copies):
        acc = proj_ref[p.zk(k), p.x].astype(F32)
        for j, copy in enumerate(row):
            copy.wait_recv()
            acc = acc + x_buf[j, k].astype(F32)
        if k:
            a_buf[k - 1] = acc.astype(BF16)
            z_copies.append(copies.start(a_buf.at[k - 1], z_buf.at[k - 1], p.device(z=p.zk(k))))
        else:
            mixed_ref[...] = acc + res_ref[...].astype(F32)
    for k in range(1, p.nz):
        z_copies[k - 1].wait_recv()
        mixed_ref[...] += z_buf[k - 1].astype(F32)
    mixed = mixed_ref[...]
    inverse = lax.rsqrt(jnp.mean(mixed * mixed, axis=1, keepdims=True) + EPSILON)
    normed = (mixed * inverse * gain_ref[...]).astype(BF16)
    width = normed.shape[1]
    own = out_ref.at[p.c, p.z, p.x, p.y]
    own[:, :width] = normed
    logits = jnp.dot(normed, router_ref[...], preferred_element_type=F32)
    sig = jax.nn.sigmoid(logits) * chosen_ref[...]
    lane = lax.broadcasted_iota(jnp.int32, sig.shape, 1)
    gates = sig / jnp.sum(jnp.where(lane < experts, sig, 0.0), axis=1, keepdims=True)
    high = gates.astype(BF16).astype(F32)
    own[:, width:] = jnp.where(lane < experts, high, gates - high).astype(BF16)

    half = width // 2
    cuts = (pl.ds(0, half), pl.ds(half, out_ref.shape[5] - half))
    a, b = cuts
    c = p.c
    z_copies = []
    for k in range(1, p.nz):
        z_copies.append(
            [
                copies.start(
                    out_ref.at[c, p.z, p.x, p.y, :, cut], out_ref.at[c, p.z, p.x, p.y, :, cut],
                    p.device(z=p.zk(k)),
                )
                for cut in cuts
            ]
        )
    first, second, core = [], [], []
    ks = list(range(p.nz))

    def spread(k):
        block = (c, p.zk(-k), p.x, p.y, slice(None))
        row = []
        for j in range(1, p.nx):
            ref = out_ref.at[block + (a,)]
            row.append(copies.start(ref, ref, p.device(x=p.xk(j))))
        for j in range(1, p.ny):
            ref = out_ref.at[block + (b,)]
            row.append(copies.start(ref, ref, p.device(y=p.yk(j))))
        return row

    def widen(k, row):
        for copy in row:
            copy.wait_recv()
        done = []
        for j in range(1, p.ny):
            ref = out_ref.at[c, p.zk(-k), :, p.y, :, a]
            done.append(copies.start(ref, ref, p.device(y=p.yk(j))))
        for j in range(1, p.nx):
            ref = out_ref.at[c, p.zk(-k), p.x, :, :, b]
            done.append(copies.start(ref, ref, p.device(x=p.xk(j))))
        return done

    def share(k, row):
        for copy in row:
            copy.wait_recv()
        ref = out_ref.at[c, p.zk(-k)]
        return copies.start(ref, ref, p.device(c=1 - c))

    for k in ks:
        if k:
            for copy in z_copies[k - 1]:
                copy.wait_recv()
        first.append(spread(k))
        if k >= 1:
            second.append(widen(k - 1, first[k - 1]))
        if k >= 2:
            core.append(share(k - 2, second[k - 2]))
    second.append(widen(ks[-1], first[-1]))
    core.append(share(ks[-2], second[-2]))
    core.append(share(ks[-1], second[-1]))
    for copy in core:
        copy.wait_recv()
    copies.finish()


def combine_kernel(
    n_seq, n_grp, in_ref, mixed_ref, out_ref,
    c_buf, acc, a1, b1, a2, b2, a3, b3, a4, b4, a5, b5, send_sems, recv_sems,
):
    p = Place(n_seq, n_grp)
    greet(axis_peers(p))
    copies = Copies(send_sems, recv_sems)
    width = out_ref.shape[1]
    half = width // 2
    a, b = pl.ds(0, half), pl.ds(half, width - half)
    order = list(range(1, p.nz)) + [0]
    core = [
        copies.start(in_ref.at[1 - p.c, p.zk(k)], c_buf.at[k], p.device(c=1 - p.c)) for k in order
    ]
    first, second, third = [], [], []

    def core_sum(i):
        k = order[i]
        core[i].wait_recv()
        for x in range(p.nx):
            for y in range(p.ny):
                acc[k, x, y] = (
                    in_ref[p.c, p.zk(k), x, y].astype(F32) + c_buf[k, x, y].astype(F32)
                ).astype(BF16)
        row = []
        for j in range(1, p.ny):
            row.append(
                copies.start(acc.at[k, :, p.yk(j), :, a], a1.at[j - 1, k], p.device(y=p.yk(j)))
            )
        for j in range(1, p.nx):
            row.append(
                copies.start(acc.at[k, p.xk(j), :, :, b], b1.at[j - 1, k], p.device(x=p.xk(j)))
            )
        first.append(row)

    def first_sum(i):
        k = order[i]
        for copy in first[i]:
            copy.wait_recv()
        for x in range(p.nx):
            total = acc[k, x, p.y, :, a].astype(F32)
            for j in range(p.ny - 1):
                total = total + a1[j, k, x].astype(F32)
            a2[k, x] = total.astype(BF16)
        for y in range(p.ny):
            total = acc[k, p.x, y, :, b].astype(F32)
            for j in range(p.nx - 1):
                total = total + b1[j, k, y].astype(F32)
            b2[k, y] = total.astype(BF16)
        row = []
        for j in range(1, p.nx):
            row.append(copies.start(a2.at[k, p.xk(j)], a3.at[j - 1, k], p.device(x=p.xk(j))))
        for j in range(1, p.ny):
            row.append(copies.start(b2.at[k, p.yk(j)], b3.at[j - 1, k], p.device(y=p.yk(j))))
        second.append(row)

    def second_sum(i):
        k = order[i]
        for copy in second[i]:
            copy.wait_recv()
        left = a2[k, p.x].astype(F32)
        for j in range(p.nx - 1):
            left = left + a3[j, k].astype(F32)
        right = b2[k, p.y].astype(F32)
        for j in range(p.ny - 1):
            right = right + b3[j, k].astype(F32)
        if k:
            a4[k - 1] = left.astype(BF16)
            b4[k - 1] = right.astype(BF16)
            third.append(copies.start(a4.at[k - 1], a5.at[k - 1], p.device(z=p.zk(k))))
            third.append(copies.start(b4.at[k - 1], b5.at[k - 1], p.device(z=p.zk(k))))
            return None
        return left, right

    n = len(order)
    for i in range(n):
        core_sum(i)
        if i >= 1:
            first_sum(i - 1)
        if i >= 2:
            second_sum(i - 2)
    first_sum(n - 1)
    second_sum(n - 2)
    left, right = second_sum(n - 1)
    left = left + mixed_ref[:, a]
    right = right + mixed_ref[:, b]
    for copy in third:
        copy.wait_recv()
    for k in range(p.nz - 1):
        left = left + a5[k].astype(F32)
        right = right + b5[k].astype(F32)
    out_ref[:, a] = left.astype(BF16)
    out_ref[:, b] = right.astype(BF16)
    copies.finish()


def expert_kernel(x_ref, gate_w_ref, up_w_ref, down_w_ref, gate_ref, out_ref, acc_ref):
    i, last = pl.program_id(1), pl.num_programs(1) - 1
    x = x_ref[:, : out_ref.shape[1]]
    gate_part = jnp.dot(x, gate_w_ref[...], preferred_element_type=F32)
    up_part = jnp.dot(x, up_w_ref[...], preferred_element_type=F32)
    act = (jax.nn.silu(gate_part) * up_part).astype(BF16)
    part = jnp.dot(act, down_w_ref[...], preferred_element_type=F32)

    @pl.when(i == 0)
    def _():
        acc_ref[...] = part

    @pl.when(i > 0)
    def _():
        acc_ref[...] += part

    @pl.when(i == last)
    def _():
        out_ref[...] = (acc_ref[...].astype(BF16).astype(F32) * gate_ref[...]).astype(BF16)


def local(
    queries, prefix_keys, prefix_values, suffix_keys, suffix_values, parents, out_proj,
    residual, norm_gain, router, routes, expert_gate, expert_up, expert_down,
):
    n_seq, n_grp = lax.axis_size("seq"), lax.axis_size("grp")
    nz, nx, ny = dims(n_seq, n_grp)
    s, g = lax.axis_index("seq"), lax.axis_index("grp")
    rows, width = queries.shape[1], queries.shape[2]
    total_rows = rows * n_seq
    keys = prefix_keys.shape[1]
    kv_width = suffix_keys.shape[2]
    group = HEADS // KVH
    own_heads = HEADS // n_seq
    own_width = own_heads * HD
    vmem = pltpu.VMEM

    packed = jnp.concatenate([queries[0], suffix_keys[0], suffix_values[0]], axis=1)
    pack_width = packed.shape[1]
    gathered = call(
        functools.partial(gather_kernel, n_seq, n_grp),
        jax.ShapeDtypeStruct((nz, nx, rows, pack_width), BF16),
        [packed], [], 0,
    ).reshape(total_rows, pack_width)

    o, m, l = pl.pallas_call(
        functools.partial(prefix_kernel, group),
        grid=(KVH,),
        in_specs=[
            pl.BlockSpec((total_rows, group * HD), lambda i: (0, i)),
            pl.BlockSpec((keys, HD), lambda i: (0, i)),
            pl.BlockSpec((keys, HD), lambda i: (0, i)),
        ],
        out_specs=[
            pl.BlockSpec((group * HD, total_rows), lambda i: (i, 0)),
            pl.BlockSpec((group, total_rows), lambda i: (i, 0)),
            pl.BlockSpec((group, total_rows), lambda i: (i, 0)),
        ],
        out_shape=[
            jax.ShapeDtypeStruct((HEADS * HD, total_rows), F32),
            jax.ShapeDtypeStruct((HEADS, total_rows), F32),
            jax.ShapeDtypeStruct((HEADS, total_rows), F32),
        ],
        compiler_params=pltpu.CompilerParams(vmem_limit_bytes=VLIMIT),
    )(gathered, prefix_keys[0], prefix_values[0])

    o_own, l_own, m_own = call(
        functools.partial(merge_kernel, n_seq, n_grp),
        [
            jax.ShapeDtypeStruct((own_width, total_rows), F32),
            jax.ShapeDtypeStruct((own_heads, total_rows), F32),
            jax.ShapeDtypeStruct((own_heads, total_rows), F32),
        ],
        [
            o.reshape(n_seq, own_width, total_rows),
            m.reshape(n_seq, own_heads, total_rows),
            l.reshape(n_seq, own_heads, total_rows),
        ],
        [
            vmem((n_seq, n_seq, own_heads, total_rows), F32),
            vmem((n_seq - 1, own_heads, total_rows), F32),
            vmem((n_seq, own_width, total_rows), BF16),
            vmem((nx - 1, nz, own_width, total_rows), BF16),
            vmem((nz - 1, own_width, total_rows), BF16),
            vmem((nz - 1, own_width, total_rows), BF16),
        ],
        1,
    )

    kv_index = s * own_heads // group
    own_q = lax.dynamic_slice_in_dim(gathered, s * own_width, own_width, 1)
    own_k = lax.dynamic_slice_in_dim(gathered, width + kv_index * HD, HD, 1)
    own_v = lax.dynamic_slice_in_dim(gathered, width + kv_width + kv_index * HD, HD, 1)
    tile = min(1024, width)
    whole = lambda *shape: pl.BlockSpec(shape, lambda i: (0,) * len(shape))
    projected = pl.pallas_call(
        functools.partial(project_kernel, own_heads),
        grid=(width // tile,),
        in_specs=[
            whole(total_rows, own_width), whole(total_rows, HD), whole(total_rows, HD),
            whole(1, total_rows), whole(own_width, total_rows), whole(own_heads, total_rows),
            whole(own_heads, total_rows), pl.BlockSpec((own_width, tile), lambda i: (0, i)),
        ],
        out_specs=pl.BlockSpec((total_rows, tile), lambda i: (0, i)),
        out_shape=jax.ShapeDtypeStruct((total_rows, width), BF16),
        scratch_shapes=[vmem((total_rows, own_width), BF16)],
        compiler_params=pltpu.CompilerParams(vmem_limit_bytes=VLIMIT),
    )(own_q, own_k, own_v, parents, o_own, l_own, m_own, out_proj)

    experts = router.shape[1]
    lanes = -(-2 * experts // 128) * 128
    chosen = jnp.sum(
        (routes[0][:, :, None] == jnp.arange(experts, dtype=jnp.int32)).astype(F32), axis=1
    )
    pad = ((0, 0), (0, lanes - 2 * experts))
    chosen = jnp.pad(jnp.concatenate([chosen, chosen], axis=1), pad)
    router_wide = jnp.pad(jnp.concatenate([router, router], axis=1), pad)
    mixed, arrived = call(
        functools.partial(norm_kernel, n_seq, n_grp, experts),
        [
            jax.ShapeDtypeStruct((rows, width), F32),
            jax.ShapeDtypeStruct((2, nz, nx, ny, rows, width + lanes), BF16),
        ],
        [
            projected.reshape(nz, nx, rows, width), residual[0], norm_gain[None], router_wide,
            chosen,
        ],
        [
            vmem((nx - 1, nz, rows, width), BF16),
            vmem((nz - 1, rows, width), BF16),
            vmem((nz - 1, rows, width), BF16),
        ],
        2,
    )

    flat = arrived.reshape(-1, width + lanes)
    parts = flat[:, width:].astype(F32)
    expert = s * n_grp + g
    lane = jnp.arange(lanes, dtype=jnp.int32)
    mine = (lane == expert) | (lane == expert + experts)
    gate = jnp.sum(jnp.where(mine[None, :], parts, 0.0), axis=1, keepdims=True)
    hidden = expert_gate.shape[2]
    row_tile, tile = min(512, flat.shape[0]), min(256, hidden)
    weighted = pl.pallas_call(
        expert_kernel,
        grid=(flat.shape[0] // row_tile, hidden // tile),
        in_specs=[
            pl.BlockSpec((row_tile, width + lanes), lambda r, i: (r, 0)),
            pl.BlockSpec((width, tile), lambda r, i: (0, i)),
            pl.BlockSpec((width, tile), lambda r, i: (0, i)),
            pl.BlockSpec((tile, width), lambda r, i: (i, 0)),
            pl.BlockSpec((row_tile, 1), lambda r, i: (r, 0)),
        ],
        out_specs=pl.BlockSpec((row_tile, width), lambda r, i: (r, 0)),
        out_shape=jax.ShapeDtypeStruct((flat.shape[0], width), BF16),
        scratch_shapes=[vmem((row_tile, width), F32)],
        compiler_params=pltpu.CompilerParams(vmem_limit_bytes=VLIMIT),
    )(flat, expert_gate[0], expert_up[0], expert_down[0], gate)

    half = width // 2
    out = call(
        functools.partial(combine_kernel, n_seq, n_grp),
        jax.ShapeDtypeStruct((rows, width), BF16),
        [weighted.reshape(2, nz, nx, ny, rows, width), mixed],
        [
            vmem((nz, nx, ny, rows, width), BF16),
            vmem((nz, nx, ny, rows, width), BF16),
            vmem((ny - 1, nz, nx, rows, half), BF16),
            vmem((nx - 1, nz, ny, rows, half), BF16),
            vmem((nz, nx, rows, half), BF16),
            vmem((nz, ny, rows, half), BF16),
            vmem((nx - 1, nz, rows, half), BF16),
            vmem((ny - 1, nz, rows, half), BF16),
            vmem((nz - 1, rows, half), BF16),
            vmem((nz - 1, rows, half), BF16),
            vmem((nz - 1, rows, half), BF16),
            vmem((nz - 1, rows, half), BF16),
        ],
        3,
    )
    return out[None]


def solution(mesh):
    in_specs = (
        P("grp", "seq", None),
        P("grp", "seq", None),
        P("grp", "seq", None),
        P("grp", "seq", None),
        P("grp", "seq", None),
        P("grp", None),
        P("seq", None),
        P("grp", "seq", None),
        P(),
        P(),
        P("grp", "seq", None),
        P(("seq", "grp"), None, None),
        P(("seq", "grp"), None, None),
        P(("seq", "grp"), None, None),
    )
    out_specs = P("grp", "seq", None)
    return jax.shard_map(local, mesh=mesh, in_specs=in_specs, out_specs=out_specs, check_vma=False)
```

```python
import functools
import math

import jax
import jax.numpy as jnp
from jax import lax
from jax.experimental import pallas as pl
from jax.experimental.pallas import tpu as pltpu
from jax.sharding import PartitionSpec as P

HEADS = 32
KVH = 4
HD = 128
DEPTH = 8
EPSILON = 1e-06
MESH = pl.DeviceIdType.MESH
SCALE = HD ** (-0.5) * math.log2(math.e)
F32 = jnp.float32
BF16 = jnp.bfloat16
VLIMIT = 60 * 1024 * 1024
SEMS = 96


class Place:
    def __init__(self, n_seq, n_grp):
        self.nx = 2 ** (int(math.log2(n_seq)) // 2)
        self.nz = n_seq // self.nx
        self.ny = n_grp // 2
        s, g = lax.axis_index("seq"), lax.axis_index("grp")
        self.z, self.x = s // self.nx, lax.rem(s, self.nx)
        self.y, self.c = g // 2, lax.rem(g, 2)

    def device(self, z=None, x=None, y=None, c=None):
        z = self.z if z is None else z
        x = self.x if x is None else x
        y = self.y if y is None else y
        c = self.c if c is None else c
        return (z * self.nx + x, y * 2 + c)

    def zk(self, k):
        return lax.rem(self.z + k + self.nz, self.nz)

    def xk(self, k):
        return lax.rem(self.x + k + self.nx, self.nx)

    def yk(self, k):
        return lax.rem(self.y + k + self.ny, self.ny)


def dims(n_seq, n_grp):
    nx = 2 ** (int(math.log2(n_seq)) // 2)
    return n_seq // nx, nx, n_grp // 2


def greet(peers):
    barrier = pltpu.get_barrier_semaphore()
    for peer in peers:
        pl.semaphore_signal(barrier, inc=1, device_id=peer, device_id_type=MESH)
    pl.semaphore_wait(barrier, len(peers))


class Copies:
    def __init__(self, send_sems, recv_sems):
        self.send_sems, self.recv_sems, self.started = send_sems, recv_sems, []

    def start(self, src, dst, device):
        n = len(self.started)
        copy = pltpu.make_async_remote_copy(
            src_ref=src,
            dst_ref=dst,
            send_sem=self.send_sems.at[n],
            recv_sem=self.recv_sems.at[n],
            device_id=device,
            device_id_type=MESH,
        )
        copy.start()
        self.started.append(copy)
        return copy

    def finish(self):
        for copy in self.started:
            copy.wait_send()


def axis_peers(p, grp=True):
    peers = [p.device(z=p.zk(k)) for k in range(1, p.nz)]
    peers += [p.device(x=p.xk(k)) for k in range(1, p.nx)]
    if grp:
        peers += [p.device(y=p.yk(k)) for k in range(1, p.ny)]
        peers += [p.device(c=1 - p.c)]
    return peers


def call(kernel, outs, ins, scratch, ident):
    vmem = pl.BlockSpec(memory_space=pltpu.VMEM)
    return pl.pallas_call(
        kernel,
        out_shape=outs,
        in_specs=[vmem] * len(ins),
        out_specs=jax.tree.map(lambda _: vmem, outs),
        scratch_shapes=list(scratch)
        + [pltpu.SemaphoreType.DMA((SEMS,)), pltpu.SemaphoreType.DMA((SEMS,))],
        compiler_params=pltpu.CompilerParams(
            collective_id=ident, has_side_effects=True, vmem_limit_bytes=VLIMIT
        ),
    )(*ins)


def gather_kernel(n_seq, n_grp, in_ref, out_ref, send_sems, recv_sems):
    p = Place(n_seq, n_grp)
    greet(axis_peers(p, grp=False))
    copies = Copies(send_sems, recv_sems)
    z_copies = [
        copies.start(in_ref, out_ref.at[p.z, p.x], p.device(z=p.zk(k))) for k in range(1, p.nz)
    ]
    x_copies = [
        copies.start(in_ref, out_ref.at[p.z, p.x], p.device(x=p.xk(j))) for j in range(1, p.nx)
    ]
    out_ref[p.z, p.x] = in_ref[...]
    for k in range(1, p.nz):
        z_copies[k - 1].wait_recv()
        block = out_ref.at[p.zk(-k), p.x]
        x_copies += [copies.start(block, block, p.device(x=p.xk(j))) for j in range(1, p.nx)]
    for copy in x_copies:
        copy.wait_recv()
    copies.finish()


def prefix_kernel(group, q_ref, k_ref, v_ref, o_ref, m_ref, l_ref):
    key, value = k_ref[...], v_ref[...]
    for h in range(group):
        s = lax.dot_general(
            key, q_ref[:, h * HD : (h + 1) * HD], (((1,), (1,)), ((), ())),
            preferred_element_type=F32,
        ) * SCALE
        m = jnp.max(s, axis=0, keepdims=True)
        w = jnp.exp2(s - m)
        l_ref[h : h + 1, :] = jnp.sum(w, axis=0, keepdims=True)
        m_ref[h : h + 1, :] = m
        o_ref[h * HD : (h + 1) * HD, :] = lax.dot_general(
            value, w.astype(BF16), (((0,), (0,)), ((), ())), preferred_element_type=F32
        )


def merge_kernel(
    n_seq, n_grp, o_ref, m_ref, l_ref, out_ref, total_ref, max_ref,
    m_buf, l_buf, s_buf, x_buf, a_buf, z_buf, send_sems, recv_sems,
):
    p = Place(n_seq, n_grp)
    s, g = lax.axis_index("seq"), lax.axis_index("grp")
    own_heads = m_ref.shape[1]
    others = [lax.rem(s + j, n_seq) for j in range(1, n_seq)]
    greet([(other, g) for other in others])
    copies = Copies(send_sems, recv_sems)
    small = []
    for j, other in enumerate(others):
        small.append(copies.start(m_ref, m_buf.at[j], (other, g)))
    for j, other in enumerate(others):
        small.append(copies.start(l_ref.at[other], l_buf.at[j], (other, g)))
    for copy in small[: n_seq - 1]:
        copy.wait_recv()
    whole = m_ref[...]
    for j in range(n_seq - 1):
        whole = jnp.maximum(whole, m_buf[j])
    x_buf_copies = []
    m_buf[n_seq - 1] = whole
    order = list(range(1, p.nz)) + [0]
    for k in order:
        row = []
        for j in list(range(1, p.nx)) + [0]:
            t = p.zk(k) * p.nx + p.xk(j)
            factor = jnp.exp2(m_ref[t] - m_buf[n_seq - 1, t])
            for h in range(own_heads):
                s_buf[t, h * HD : (h + 1) * HD, :] = (
                    o_ref[t, h * HD : (h + 1) * HD, :] * factor[h : h + 1, :]
                ).astype(BF16)
            if j:
                row.append(
                    copies.start(s_buf.at[t], x_buf.at[j - 1, k], p.device(x=p.xk(j)))
                )
        x_buf_copies.append(row)
    z_copies = []
    last = None
    for k, row in zip(order, x_buf_copies):
        t = p.zk(k) * p.nx + p.x
        acc = s_buf[t].astype(F32)
        for j, copy in enumerate(row):
            copy.wait_recv()
            acc = acc + x_buf[j, k].astype(F32)
        if k:
            a_buf[k - 1] = acc.astype(BF16)
            z_copies.append(copies.start(a_buf.at[k - 1], z_buf.at[k - 1], p.device(z=p.zk(k))))
        else:
            last = acc
    out_ref[...] = last
    for copy in small[n_seq - 1 :]:
        copy.wait_recv()
    own_max = m_buf[n_seq - 1, s]
    total = l_ref[s] * jnp.exp2(m_ref[s] - own_max)
    for j in range(n_seq - 1):
        total = total + l_buf[j] * jnp.exp2(m_buf[j, s] - own_max)
    total_ref[...] = total
    max_ref[...] = own_max
    for k in range(1, p.nz):
        z_copies[k - 1].wait_recv()
        out_ref[...] += z_buf[k - 1].astype(F32)
    copies.finish()


def project_kernel(own_heads, q_ref, k_ref, v_ref, par_ref, o_ref, l_ref, m_ref, w_ref, out_ref, att_ref):
    rows = q_ref.shape[0]

    @pl.when(pl.program_id(0) == 0)
    def _():
        j_index = lax.broadcasted_iota(jnp.int32, (rows, rows), 0)
        i_index = lax.broadcasted_iota(jnp.int32, (rows, rows), 1)
        step = (par_ref[...] == j_index).astype(F32) + (i_index == j_index).astype(F32)
        paths, power = step, step
        for _ in range(int(math.log2(DEPTH)) - 1):
            power = jnp.dot(power.astype(BF16), power.astype(BF16), preferred_element_type=F32)
            paths = jnp.dot(paths.astype(BF16), power.astype(BF16), preferred_element_type=F32)
        seen = paths > 0.5
        for h in range(own_heads):
            s = lax.dot_general(
                k_ref[...], q_ref[:, h * HD : (h + 1) * HD], (((1,), (1,)), ((), ())),
                preferred_element_type=F32,
            ) * SCALE
            s = jnp.where(seen, s, -jnp.inf)
            before = m_ref[h : h + 1, :]
            top = jnp.maximum(before, jnp.max(s, axis=0, keepdims=True))
            w = jnp.exp2(s - top)
            scale = jnp.exp2(before - top)
            total = l_ref[h : h + 1, :] * scale + jnp.sum(w, axis=0, keepdims=True)
            o = lax.dot_general(
                v_ref[...], w.astype(BF16), (((0,), (0,)), ((), ())), preferred_element_type=F32
            )
            o = (o_ref[h * HD : (h + 1) * HD, :] * scale + o) / total
            att_ref[:, h * HD : (h + 1) * HD] = o.T.astype(BF16)

    out_ref[...] = jnp.dot(att_ref[...], w_ref[...], preferred_element_type=F32).astype(BF16)


def norm_kernel(
    n_seq, n_grp, experts, proj_ref, res_ref, gain_ref, router_ref, chosen_ref,
    mixed_ref, out_ref, x_buf, a_buf, z_buf, send_sems, recv_sems,
):
    p = Place(n_seq, n_grp)
    greet(axis_peers(p))
    copies = Copies(send_sems, recv_sems)
    order = list(range(1, p.nz)) + [0]
    x_copies = [
        [
            copies.start(proj_ref.at[p.zk(k), p.xk(j)], x_buf.at[j - 1, k], p.device(x=p.xk(j)))
            for j in range(1, p.nx)
        ]
        for k in order
    ]
    z_copies = []
    mixed = None
    for k, row in zip(order, x_copies):
        acc = proj_ref[p.zk(k), p.x].astype(F32)
        for j, copy in enumerate(row):
            copy.wait_recv()
            acc = acc + x_buf[j, k].astype(F32)
        if k:
            a_buf[k - 1] = acc.astype(BF16)
            z_copies.append(copies.start(a_buf.at[k - 1], z_buf.at[k - 1], p.device(z=p.zk(k))))
        else:
            mixed_ref[...] = acc + res_ref[...].astype(F32)
    for k in range(1, p.nz):
        z_copies[k - 1].wait_recv()
        mixed_ref[...] += z_buf[k - 1].astype(F32)
    mixed = mixed_ref[...]
    inverse = lax.rsqrt(jnp.mean(mixed * mixed, axis=1, keepdims=True) + EPSILON)
    normed = (mixed * inverse * gain_ref[...]).astype(BF16)
    width = normed.shape[1]
    own = out_ref.at[p.c, p.z, p.x, p.y]
    own[:, :width] = normed
    logits = jnp.dot(normed, router_ref[...], preferred_element_type=F32)
    sig = jax.nn.sigmoid(logits) * chosen_ref[...]
    lane = lax.broadcasted_iota(jnp.int32, sig.shape, 1)
    gates = sig / jnp.sum(jnp.where(lane < experts, sig, 0.0), axis=1, keepdims=True)
    high = gates.astype(BF16).astype(F32)
    own[:, width:] = jnp.where(lane < experts, high, gates - high).astype(BF16)

    half = width // 2
    cuts = (pl.ds(0, half), pl.ds(half, out_ref.shape[5] - half))
    a, b = cuts
    c = p.c
    z_copies = []
    for k in range(1, p.nz):
        z_copies.append(
            [
                copies.start(
                    out_ref.at[c, p.z, p.x, p.y, :, cut], out_ref.at[c, p.z, p.x, p.y, :, cut],
                    p.device(z=p.zk(k)),
                )
                for cut in cuts
            ]
        )
    first, second, core = [], [], []
    ks = list(range(p.nz))

    def spread(k):
        block = (c, p.zk(-k), p.x, p.y, slice(None))
        row = []
        for j in range(1, p.nx):
            ref = out_ref.at[block + (a,)]
            row.append(copies.start(ref, ref, p.device(x=p.xk(j))))
        for j in range(1, p.ny):
            ref = out_ref.at[block + (b,)]
            row.append(copies.start(ref, ref, p.device(y=p.yk(j))))
        return row

    def widen(k, row):
        for copy in row:
            copy.wait_recv()
        done = []
        for j in range(1, p.ny):
            ref = out_ref.at[c, p.zk(-k), :, p.y, :, a]
            done.append(copies.start(ref, ref, p.device(y=p.yk(j))))
        for j in range(1, p.nx):
            ref = out_ref.at[c, p.zk(-k), p.x, :, :, b]
            done.append(copies.start(ref, ref, p.device(x=p.xk(j))))
        return done

    def share(k, row):
        for copy in row:
            copy.wait_recv()
        ref = out_ref.at[c, p.zk(-k)]
        return copies.start(ref, ref, p.device(c=1 - c))

    for k in ks:
        if k:
            for copy in z_copies[k - 1]:
                copy.wait_recv()
        first.append(spread(k))
        if k >= 1:
            second.append(widen(k - 1, first[k - 1]))
        if k >= 2:
            core.append(share(k - 2, second[k - 2]))
    second.append(widen(ks[-1], first[-1]))
    core.append(share(ks[-2], second[-2]))
    core.append(share(ks[-1], second[-1]))
    for copy in core:
        copy.wait_recv()
    copies.finish()


def combine_kernel(
    n_seq, n_grp, in_ref, mixed_ref, out_ref,
    c_buf, acc, a1, b1, a2, b2, a3, b3, a4, b4, a5, b5, send_sems, recv_sems,
):
    p = Place(n_seq, n_grp)
    greet(axis_peers(p))
    copies = Copies(send_sems, recv_sems)
    width = out_ref.shape[1]
    half = width // 2
    a, b = pl.ds(0, half), pl.ds(half, width - half)
    order = list(range(1, p.nz)) + [0]
    core = [
        copies.start(in_ref.at[1 - p.c, p.zk(k)], c_buf.at[k], p.device(c=1 - p.c)) for k in order
    ]
    first, second, third = [], [], []

    def core_sum(i):
        k = order[i]
        core[i].wait_recv()
        for x in range(p.nx):
            for y in range(p.ny):
                acc[k, x, y] = (
                    in_ref[p.c, p.zk(k), x, y].astype(F32) + c_buf[k, x, y].astype(F32)
                ).astype(BF16)
        row = []
        for j in range(1, p.ny):
            row.append(
                copies.start(acc.at[k, :, p.yk(j), :, a], a1.at[j - 1, k], p.device(y=p.yk(j)))
            )
        for j in range(1, p.nx):
            row.append(
                copies.start(acc.at[k, p.xk(j), :, :, b], b1.at[j - 1, k], p.device(x=p.xk(j)))
            )
        first.append(row)

    def first_sum(i):
        k = order[i]
        for copy in first[i]:
            copy.wait_recv()
        for x in range(p.nx):
            total = acc[k, x, p.y, :, a].astype(F32)
            for j in range(p.ny - 1):
                total = total + a1[j, k, x].astype(F32)
            a2[k, x] = total.astype(BF16)
        for y in range(p.ny):
            total = acc[k, p.x, y, :, b].astype(F32)
            for j in range(p.nx - 1):
                total = total + b1[j, k, y].astype(F32)
            b2[k, y] = total.astype(BF16)
        row = []
        for j in range(1, p.nx):
            row.append(copies.start(a2.at[k, p.xk(j)], a3.at[j - 1, k], p.device(x=p.xk(j))))
        for j in range(1, p.ny):
            row.append(copies.start(b2.at[k, p.yk(j)], b3.at[j - 1, k], p.device(y=p.yk(j))))
        second.append(row)

    def second_sum(i):
        k = order[i]
        for copy in second[i]:
            copy.wait_recv()
        left = a2[k, p.x].astype(F32)
        for j in range(p.nx - 1):
            left = left + a3[j, k].astype(F32)
        right = b2[k, p.y].astype(F32)
        for j in range(p.ny - 1):
            right = right + b3[j, k].astype(F32)
        if k:
            a4[k - 1] = left.astype(BF16)
            b4[k - 1] = right.astype(BF16)
            third.append(copies.start(a4.at[k - 1], a5.at[k - 1], p.device(z=p.zk(k))))
            third.append(copies.start(b4.at[k - 1], b5.at[k - 1], p.device(z=p.zk(k))))
            return None
        return left, right

    n = len(order)
    for i in range(n):
        core_sum(i)
        if i >= 1:
            first_sum(i - 1)
        if i >= 2:
            second_sum(i - 2)
    first_sum(n - 1)
    second_sum(n - 2)
    left, right = second_sum(n - 1)
    left = left + mixed_ref[:, a]
    right = right + mixed_ref[:, b]
    for copy in third:
        copy.wait_recv()
    for k in range(p.nz - 1):
        left = left + a5[k].astype(F32)
        right = right + b5[k].astype(F32)
    out_ref[:, a] = left.astype(BF16)
    out_ref[:, b] = right.astype(BF16)
    copies.finish()


def expert_kernel(x_ref, gate_w_ref, up_w_ref, down_w_ref, gate_ref, out_ref, acc_ref):
    i, last = pl.program_id(1), pl.num_programs(1) - 1
    x = x_ref[:, : out_ref.shape[1]]
    gate_part = jnp.dot(x, gate_w_ref[...], preferred_element_type=F32)
    up_part = jnp.dot(x, up_w_ref[...], preferred_element_type=F32)
    act = (jax.nn.silu(gate_part) * up_part).astype(BF16)
    part = jnp.dot(act, down_w_ref[...], preferred_element_type=F32)

    @pl.when(i == 0)
    def _():
        acc_ref[...] = part

    @pl.when(i > 0)
    def _():
        acc_ref[...] += part

    @pl.when(i == last)
    def _():
        out_ref[...] = (acc_ref[...].astype(BF16).astype(F32) * gate_ref[...]).astype(BF16)


def local(
    queries, prefix_keys, prefix_values, suffix_keys, suffix_values, parents, out_proj,
    residual, norm_gain, router, routes, expert_gate, expert_up, expert_down,
):
    n_seq, n_grp = lax.axis_size("seq"), lax.axis_size("grp")
    nz, nx, ny = dims(n_seq, n_grp)
    s, g = lax.axis_index("seq"), lax.axis_index("grp")
    rows, width = queries.shape[1], queries.shape[2]
    total_rows = rows * n_seq
    keys = prefix_keys.shape[1]
    kv_width = suffix_keys.shape[2]
    group = HEADS // KVH
    own_heads = HEADS // n_seq
    own_width = own_heads * HD
    vmem = pltpu.VMEM

    packed = jnp.concatenate([queries[0], suffix_keys[0], suffix_values[0]], axis=1)
    pack_width = packed.shape[1]
    gathered = call(
        functools.partial(gather_kernel, n_seq, n_grp),
        jax.ShapeDtypeStruct((nz, nx, rows, pack_width), BF16),
        [packed], [], 0,
    ).reshape(total_rows, pack_width)

    o, m, l = pl.pallas_call(
        functools.partial(prefix_kernel, group),
        grid=(KVH,),
        in_specs=[
            pl.BlockSpec((total_rows, group * HD), lambda i: (0, i)),
            pl.BlockSpec((keys, HD), lambda i: (0, i)),
            pl.BlockSpec((keys, HD), lambda i: (0, i)),
        ],
        out_specs=[
            pl.BlockSpec((group * HD, total_rows), lambda i: (i, 0)),
            pl.BlockSpec((group, total_rows), lambda i: (i, 0)),
            pl.BlockSpec((group, total_rows), lambda i: (i, 0)),
        ],
        out_shape=[
            jax.ShapeDtypeStruct((HEADS * HD, total_rows), F32),
            jax.ShapeDtypeStruct((HEADS, total_rows), F32),
            jax.ShapeDtypeStruct((HEADS, total_rows), F32),
        ],
        compiler_params=pltpu.CompilerParams(vmem_limit_bytes=VLIMIT),
    )(gathered, prefix_keys[0], prefix_values[0])

    o_own, l_own, m_own = call(
        functools.partial(merge_kernel, n_seq, n_grp),
        [
            jax.ShapeDtypeStruct((own_width, total_rows), F32),
            jax.ShapeDtypeStruct((own_heads, total_rows), F32),
            jax.ShapeDtypeStruct((own_heads, total_rows), F32),
        ],
        [
            o.reshape(n_seq, own_width, total_rows),
            m.reshape(n_seq, own_heads, total_rows),
            l.reshape(n_seq, own_heads, total_rows),
        ],
        [
            vmem((n_seq, n_seq, own_heads, total_rows), F32),
            vmem((n_seq - 1, own_heads, total_rows), F32),
            vmem((n_seq, own_width, total_rows), BF16),
            vmem((nx - 1, nz, own_width, total_rows), BF16),
            vmem((nz - 1, own_width, total_rows), BF16),
            vmem((nz - 1, own_width, total_rows), BF16),
        ],
        1,
    )

    kv_index = s * own_heads // group
    own_q = lax.dynamic_slice_in_dim(gathered, s * own_width, own_width, 1)
    own_k = lax.dynamic_slice_in_dim(gathered, width + kv_index * HD, HD, 1)
    own_v = lax.dynamic_slice_in_dim(gathered, width + kv_width + kv_index * HD, HD, 1)
    tile = min(1024, width)
    whole = lambda *shape: pl.BlockSpec(shape, lambda i: (0,) * len(shape))
    projected = pl.pallas_call(
        functools.partial(project_kernel, own_heads),
        grid=(width // tile,),
        in_specs=[
            whole(total_rows, own_width), whole(total_rows, HD), whole(total_rows, HD),
            whole(1, total_rows), whole(own_width, total_rows), whole(own_heads, total_rows),
            whole(own_heads, total_rows), pl.BlockSpec((own_width, tile), lambda i: (0, i)),
        ],
        out_specs=pl.BlockSpec((total_rows, tile), lambda i: (0, i)),
        out_shape=jax.ShapeDtypeStruct((total_rows, width), BF16),
        scratch_shapes=[vmem((total_rows, own_width), BF16)],
        compiler_params=pltpu.CompilerParams(vmem_limit_bytes=VLIMIT),
    )(own_q, own_k, own_v, parents, o_own, l_own, m_own, out_proj)

    experts = router.shape[1]
    lanes = -(-2 * experts // 128) * 128
    chosen = jnp.sum(
        (routes[0][:, :, None] == jnp.arange(experts, dtype=jnp.int32)).astype(F32), axis=1
    )
    pad = ((0, 0), (0, lanes - 2 * experts))
    chosen = jnp.pad(jnp.concatenate([chosen, chosen], axis=1), pad)
    router_wide = jnp.pad(jnp.concatenate([router, router], axis=1), pad)
    mixed, arrived = call(
        functools.partial(norm_kernel, n_seq, n_grp, experts),
        [
            jax.ShapeDtypeStruct((rows, width), F32),
            jax.ShapeDtypeStruct((2, nz, nx, ny, rows, width + lanes), BF16),
        ],
        [
            projected.reshape(nz, nx, rows, width), residual[0], norm_gain[None], router_wide,
            chosen,
        ],
        [
            vmem((nx - 1, nz, rows, width), BF16),
            vmem((nz - 1, rows, width), BF16),
            vmem((nz - 1, rows, width), BF16),
        ],
        2,
    )

    flat = arrived.reshape(-1, width + lanes)
    parts = flat[:, width:].astype(F32)
    expert = s * n_grp + g
    lane = jnp.arange(lanes, dtype=jnp.int32)
    mine = (lane == expert) | (lane == expert + experts)
    gate = jnp.sum(jnp.where(mine[None, :], parts, 0.0), axis=1, keepdims=True)
    hidden = expert_gate.shape[2]
    row_tile, tile = min(512, flat.shape[0]), min(384, hidden)
    weighted = pl.pallas_call(
        expert_kernel,
        grid=(flat.shape[0] // row_tile, hidden // tile),
        in_specs=[
            pl.BlockSpec((row_tile, width + lanes), lambda r, i: (r, 0)),
            pl.BlockSpec((width, tile), lambda r, i: (0, i)),
            pl.BlockSpec((width, tile), lambda r, i: (0, i)),
            pl.BlockSpec((tile, width), lambda r, i: (i, 0)),
            pl.BlockSpec((row_tile, 1), lambda r, i: (r, 0)),
        ],
        out_specs=pl.BlockSpec((row_tile, width), lambda r, i: (r, 0)),
        out_shape=jax.ShapeDtypeStruct((flat.shape[0], width), BF16),
        scratch_shapes=[vmem((row_tile, width), F32)],
        compiler_params=pltpu.CompilerParams(vmem_limit_bytes=VLIMIT),
    )(flat, expert_gate[0], expert_up[0], expert_down[0], gate)

    half = width // 2
    out = call(
        functools.partial(combine_kernel, n_seq, n_grp),
        jax.ShapeDtypeStruct((rows, width), BF16),
        [weighted.reshape(2, nz, nx, ny, rows, width), mixed],
        [
            vmem((nz, nx, ny, rows, width), BF16),
            vmem((nz, nx, ny, rows, width), BF16),
            vmem((ny - 1, nz, nx, rows, half), BF16),
            vmem((nx - 1, nz, ny, rows, half), BF16),
            vmem((nz, nx, rows, half), BF16),
            vmem((nz, ny, rows, half), BF16),
            vmem((nx - 1, nz, rows, half), BF16),
            vmem((ny - 1, nz, rows, half), BF16),
            vmem((nz - 1, rows, half), BF16),
            vmem((nz - 1, rows, half), BF16),
            vmem((nz - 1, rows, half), BF16),
            vmem((nz - 1, rows, half), BF16),
        ],
        3,
    )
    return out[None]


def solution(mesh):
    in_specs = (
        P("grp", "seq", None),
        P("grp", "seq", None),
        P("grp", "seq", None),
        P("grp", "seq", None),
        P("grp", "seq", None),
        P("grp", None),
        P("seq", None),
        P("grp", "seq", None),
        P(),
        P(),
        P("grp", "seq", None),
        P(("seq", "grp"), None, None),
        P(("seq", "grp"), None, None),
        P(("seq", "grp"), None, None),
    )
    out_specs = P("grp", "seq", None)
    return jax.shard_map(local, mesh=mesh, in_specs=in_specs, out_specs=out_specs, check_vma=False)
```

```python
import functools
import math

import jax
import jax.numpy as jnp
from jax import lax
from jax.experimental import pallas as pl
from jax.experimental.pallas import tpu as pltpu
from jax.sharding import PartitionSpec as P

HEADS = 32
KVH = 4
HD = 128
DEPTH = 8
EPSILON = 1e-06
MESH = pl.DeviceIdType.MESH
SCALE = HD ** (-0.5) * math.log2(math.e)
F32 = jnp.float32
BF16 = jnp.bfloat16
VLIMIT = 60 * 1024 * 1024
SEMS = 96


class Place:
    def __init__(self, n_seq, n_grp):
        self.nx = 2 ** (int(math.log2(n_seq)) // 2)
        self.nz = n_seq // self.nx
        self.ny = n_grp // 2
        s, g = lax.axis_index("seq"), lax.axis_index("grp")
        self.z, self.x = s // self.nx, lax.rem(s, self.nx)
        self.y, self.c = g // 2, lax.rem(g, 2)

    def device(self, z=None, x=None, y=None, c=None):
        z = self.z if z is None else z
        x = self.x if x is None else x
        y = self.y if y is None else y
        c = self.c if c is None else c
        return (z * self.nx + x, y * 2 + c)

    def zk(self, k):
        return lax.rem(self.z + k + self.nz, self.nz)

    def xk(self, k):
        return lax.rem(self.x + k + self.nx, self.nx)

    def yk(self, k):
        return lax.rem(self.y + k + self.ny, self.ny)


def dims(n_seq, n_grp):
    nx = 2 ** (int(math.log2(n_seq)) // 2)
    return n_seq // nx, nx, n_grp // 2


def greet(peers):
    barrier = pltpu.get_barrier_semaphore()
    for peer in peers:
        pl.semaphore_signal(barrier, inc=1, device_id=peer, device_id_type=MESH)
    pl.semaphore_wait(barrier, len(peers))


class Copies:
    def __init__(self, send_sems, recv_sems):
        self.send_sems, self.recv_sems, self.started = send_sems, recv_sems, []

    def start(self, src, dst, device):
        n = len(self.started)
        copy = pltpu.make_async_remote_copy(
            src_ref=src,
            dst_ref=dst,
            send_sem=self.send_sems.at[n],
            recv_sem=self.recv_sems.at[n],
            device_id=device,
            device_id_type=MESH,
        )
        copy.start()
        self.started.append(copy)
        return copy

    def finish(self):
        for copy in self.started:
            copy.wait_send()


def axis_peers(p, grp=True):
    peers = [p.device(z=p.zk(k)) for k in range(1, p.nz)]
    peers += [p.device(x=p.xk(k)) for k in range(1, p.nx)]
    if grp:
        peers += [p.device(y=p.yk(k)) for k in range(1, p.ny)]
        peers += [p.device(c=1 - p.c)]
    return peers


def call(kernel, outs, ins, scratch, ident):
    vmem = pl.BlockSpec(memory_space=pltpu.VMEM)
    return pl.pallas_call(
        kernel,
        out_shape=outs,
        in_specs=[vmem] * len(ins),
        out_specs=jax.tree.map(lambda _: vmem, outs),
        scratch_shapes=list(scratch)
        + [pltpu.SemaphoreType.DMA((SEMS,)), pltpu.SemaphoreType.DMA((SEMS,))],
        compiler_params=pltpu.CompilerParams(
            collective_id=ident, has_side_effects=True, vmem_limit_bytes=VLIMIT
        ),
    )(*ins)


def gather_kernel(n_seq, n_grp, in_ref, out_ref, send_sems, recv_sems):
    p = Place(n_seq, n_grp)
    greet(axis_peers(p, grp=False))
    copies = Copies(send_sems, recv_sems)
    z_copies = [
        copies.start(in_ref, out_ref.at[p.z, p.x], p.device(z=p.zk(k))) for k in range(1, p.nz)
    ]
    x_copies = [
        copies.start(in_ref, out_ref.at[p.z, p.x], p.device(x=p.xk(j))) for j in range(1, p.nx)
    ]
    out_ref[p.z, p.x] = in_ref[...]
    for k in range(1, p.nz):
        z_copies[k - 1].wait_recv()
        block = out_ref.at[p.zk(-k), p.x]
        x_copies += [copies.start(block, block, p.device(x=p.xk(j))) for j in range(1, p.nx)]
    for copy in x_copies:
        copy.wait_recv()
    copies.finish()


def prefix_kernel(group, q_ref, k_ref, v_ref, o_ref, m_ref, l_ref):
    key, value = k_ref[...], v_ref[...]
    for h in range(group):
        s = lax.dot_general(
            key, q_ref[:, h * HD : (h + 1) * HD], (((1,), (1,)), ((), ())),
            preferred_element_type=F32,
        ) * SCALE
        m = jnp.max(s, axis=0, keepdims=True)
        w = jnp.exp2(s - m)
        l_ref[h : h + 1, :] = jnp.sum(w, axis=0, keepdims=True)
        m_ref[h : h + 1, :] = m
        o_ref[h * HD : (h + 1) * HD, :] = lax.dot_general(
            value, w.astype(BF16), (((0,), (0,)), ((), ())), preferred_element_type=F32
        )


def merge_kernel(
    n_seq, n_grp, o_ref, m_ref, l_ref, out_ref, total_ref, max_ref,
    m_buf, l_buf, s_buf, x_buf, a_buf, z_buf, send_sems, recv_sems,
):
    p = Place(n_seq, n_grp)
    s, g = lax.axis_index("seq"), lax.axis_index("grp")
    own_heads = m_ref.shape[1]
    others = [lax.rem(s + j, n_seq) for j in range(1, n_seq)]
    greet([(other, g) for other in others])
    copies = Copies(send_sems, recv_sems)
    small = []
    for j, other in enumerate(others):
        small.append(copies.start(m_ref, m_buf.at[j], (other, g)))
    for j, other in enumerate(others):
        small.append(copies.start(l_ref.at[other], l_buf.at[j], (other, g)))
    for copy in small[: n_seq - 1]:
        copy.wait_recv()
    whole = m_ref[...]
    for j in range(n_seq - 1):
        whole = jnp.maximum(whole, m_buf[j])
    x_buf_copies = []
    m_buf[n_seq - 1] = whole
    order = list(range(1, p.nz)) + [0]
    for k in order:
        row = []
        for j in list(range(1, p.nx)) + [0]:
            t = p.zk(k) * p.nx + p.xk(j)
            factor = jnp.exp2(m_ref[t] - m_buf[n_seq - 1, t])
            for h in range(own_heads):
                s_buf[t, h * HD : (h + 1) * HD, :] = (
                    o_ref[t, h * HD : (h + 1) * HD, :] * factor[h : h + 1, :]
                ).astype(BF16)
            if j:
                row.append(
                    copies.start(s_buf.at[t], x_buf.at[j - 1, k], p.device(x=p.xk(j)))
                )
        x_buf_copies.append(row)
    z_copies = []
    last = None
    for k, row in zip(order, x_buf_copies):
        t = p.zk(k) * p.nx + p.x
        acc = s_buf[t].astype(F32)
        for j, copy in enumerate(row):
            copy.wait_recv()
            acc = acc + x_buf[j, k].astype(F32)
        if k:
            a_buf[k - 1] = acc.astype(BF16)
            z_copies.append(copies.start(a_buf.at[k - 1], z_buf.at[k - 1], p.device(z=p.zk(k))))
        else:
            last = acc
    out_ref[...] = last
    for copy in small[n_seq - 1 :]:
        copy.wait_recv()
    own_max = m_buf[n_seq - 1, s]
    total = l_ref[s] * jnp.exp2(m_ref[s] - own_max)
    for j in range(n_seq - 1):
        total = total + l_buf[j] * jnp.exp2(m_buf[j, s] - own_max)
    total_ref[...] = total
    max_ref[...] = own_max
    for k in range(1, p.nz):
        z_copies[k - 1].wait_recv()
        out_ref[...] += z_buf[k - 1].astype(F32)
    copies.finish()


def project_kernel(own_heads, q_ref, k_ref, v_ref, par_ref, o_ref, l_ref, m_ref, w_ref, out_ref, att_ref):
    rows = q_ref.shape[0]

    @pl.when(pl.program_id(0) == 0)
    def _():
        j_index = lax.broadcasted_iota(jnp.int32, (rows, rows), 0)
        i_index = lax.broadcasted_iota(jnp.int32, (rows, rows), 1)
        step = (par_ref[...] == j_index).astype(F32) + (i_index == j_index).astype(F32)
        paths, power = step, step
        for _ in range(int(math.log2(DEPTH)) - 1):
            power = jnp.dot(power.astype(BF16), power.astype(BF16), preferred_element_type=F32)
            paths = jnp.dot(paths.astype(BF16), power.astype(BF16), preferred_element_type=F32)
        seen = paths > 0.5
        for h in range(own_heads):
            s = lax.dot_general(
                k_ref[...], q_ref[:, h * HD : (h + 1) * HD], (((1,), (1,)), ((), ())),
                preferred_element_type=F32,
            ) * SCALE
            s = jnp.where(seen, s, -jnp.inf)
            before = m_ref[h : h + 1, :]
            top = jnp.maximum(before, jnp.max(s, axis=0, keepdims=True))
            w = jnp.exp2(s - top)
            scale = jnp.exp2(before - top)
            total = l_ref[h : h + 1, :] * scale + jnp.sum(w, axis=0, keepdims=True)
            o = lax.dot_general(
                v_ref[...], w.astype(BF16), (((0,), (0,)), ((), ())), preferred_element_type=F32
            )
            o = (o_ref[h * HD : (h + 1) * HD, :] * scale + o) / total
            att_ref[:, h * HD : (h + 1) * HD] = o.T.astype(BF16)

    out_ref[...] = jnp.dot(att_ref[...], w_ref[...], preferred_element_type=F32).astype(BF16)


def norm_kernel(
    n_seq, n_grp, experts, proj_ref, res_ref, gain_ref, router_ref, chosen_ref,
    mixed_ref, out_ref, x_buf, a_buf, z_buf, send_sems, recv_sems,
):
    p = Place(n_seq, n_grp)
    greet(axis_peers(p))
    copies = Copies(send_sems, recv_sems)
    order = list(range(1, p.nz)) + [0]
    x_copies = [
        [
            copies.start(proj_ref.at[p.zk(k), p.xk(j)], x_buf.at[j - 1, k], p.device(x=p.xk(j)))
            for j in range(1, p.nx)
        ]
        for k in order
    ]
    z_copies = []
    mixed = None
    for k, row in zip(order, x_copies):
        acc = proj_ref[p.zk(k), p.x].astype(F32)
        for j, copy in enumerate(row):
            copy.wait_recv()
            acc = acc + x_buf[j, k].astype(F32)
        if k:
            a_buf[k - 1] = acc.astype(BF16)
            z_copies.append(copies.start(a_buf.at[k - 1], z_buf.at[k - 1], p.device(z=p.zk(k))))
        else:
            mixed_ref[...] = acc + res_ref[...].astype(F32)
    for k in range(1, p.nz):
        z_copies[k - 1].wait_recv()
        mixed_ref[...] += z_buf[k - 1].astype(F32)
    mixed = mixed_ref[...]
    inverse = lax.rsqrt(jnp.mean(mixed * mixed, axis=1, keepdims=True) + EPSILON)
    normed = (mixed * inverse * gain_ref[...]).astype(BF16)
    width = normed.shape[1]
    own = out_ref.at[p.c, p.z, p.x, p.y]
    own[:, :width] = normed
    logits = jnp.dot(normed, router_ref[...], preferred_element_type=F32)
    sig = jax.nn.sigmoid(logits) * chosen_ref[...]
    lane = lax.broadcasted_iota(jnp.int32, sig.shape, 1)
    gates = sig / jnp.sum(jnp.where(lane < experts, sig, 0.0), axis=1, keepdims=True)
    high = gates.astype(BF16).astype(F32)
    own[:, width:] = jnp.where(lane < experts, high, gates - high).astype(BF16)

    half = width // 2
    cuts = (pl.ds(0, half), pl.ds(half, out_ref.shape[5] - half))
    a, b = cuts
    c = p.c
    z_copies = []
    for k in range(1, p.nz):
        z_copies.append(
            [
                copies.start(
                    out_ref.at[c, p.z, p.x, p.y, :, cut], out_ref.at[c, p.z, p.x, p.y, :, cut],
                    p.device(z=p.zk(k)),
                )
                for cut in cuts
            ]
        )
    first, second, core = [], [], []
    ks = list(range(p.nz))

    def spread(k):
        block = (c, p.zk(-k), p.x, p.y, slice(None))
        row = []
        for j in range(1, p.nx):
            ref = out_ref.at[block + (a,)]
            row.append(copies.start(ref, ref, p.device(x=p.xk(j))))
        for j in range(1, p.ny):
            ref = out_ref.at[block + (b,)]
            row.append(copies.start(ref, ref, p.device(y=p.yk(j))))
        return row

    def widen(k, row):
        for copy in row:
            copy.wait_recv()
        done = []
        for j in range(1, p.ny):
            ref = out_ref.at[c, p.zk(-k), :, p.y, :, a]
            done.append(copies.start(ref, ref, p.device(y=p.yk(j))))
        for j in range(1, p.nx):
            ref = out_ref.at[c, p.zk(-k), p.x, :, :, b]
            done.append(copies.start(ref, ref, p.device(x=p.xk(j))))
        return done

    def share(k, row):
        for copy in row:
            copy.wait_recv()
        ref = out_ref.at[c, p.zk(-k)]
        return copies.start(ref, ref, p.device(c=1 - c))

    for k in ks:
        if k:
            for copy in z_copies[k - 1]:
                copy.wait_recv()
        first.append(spread(k))
        if k >= 1:
            second.append(widen(k - 1, first[k - 1]))
        if k >= 2:
            core.append(share(k - 2, second[k - 2]))
    second.append(widen(ks[-1], first[-1]))
    core.append(share(ks[-2], second[-2]))
    core.append(share(ks[-1], second[-1]))
    for copy in core:
        copy.wait_recv()
    copies.finish()


def combine_kernel(
    n_seq, n_grp, in_ref, mixed_ref, out_ref,
    c_buf, acc, a1, b1, a2, b2, a3, b3, a4, b4, a5, b5, send_sems, recv_sems,
):
    p = Place(n_seq, n_grp)
    greet(axis_peers(p))
    copies = Copies(send_sems, recv_sems)
    width = out_ref.shape[1]
    half = width // 2
    a, b = pl.ds(0, half), pl.ds(half, width - half)
    order = list(range(1, p.nz)) + [0]
    core = [
        copies.start(in_ref.at[1 - p.c, p.zk(k)], c_buf.at[k], p.device(c=1 - p.c)) for k in order
    ]
    first, second, third = [], [], []

    def core_sum(i):
        k = order[i]
        core[i].wait_recv()
        for x in range(p.nx):
            for y in range(p.ny):
                acc[k, x, y] = (
                    in_ref[p.c, p.zk(k), x, y].astype(F32) + c_buf[k, x, y].astype(F32)
                ).astype(BF16)
        row = []
        for j in range(1, p.ny):
            row.append(
                copies.start(acc.at[k, :, p.yk(j), :, a], a1.at[j - 1, k], p.device(y=p.yk(j)))
            )
        for j in range(1, p.nx):
            row.append(
                copies.start(acc.at[k, p.xk(j), :, :, b], b1.at[j - 1, k], p.device(x=p.xk(j)))
            )
        first.append(row)

    def first_sum(i):
        k = order[i]
        for copy in first[i]:
            copy.wait_recv()
        for x in range(p.nx):
            total = acc[k, x, p.y, :, a].astype(F32)
            for j in range(p.ny - 1):
                total = total + a1[j, k, x].astype(F32)
            a2[k, x] = total.astype(BF16)
        for y in range(p.ny):
            total = acc[k, p.x, y, :, b].astype(F32)
            for j in range(p.nx - 1):
                total = total + b1[j, k, y].astype(F32)
            b2[k, y] = total.astype(BF16)
        row = []
        for j in range(1, p.nx):
            row.append(copies.start(a2.at[k, p.xk(j)], a3.at[j - 1, k], p.device(x=p.xk(j))))
        for j in range(1, p.ny):
            row.append(copies.start(b2.at[k, p.yk(j)], b3.at[j - 1, k], p.device(y=p.yk(j))))
        second.append(row)

    def second_sum(i):
        k = order[i]
        for copy in second[i]:
            copy.wait_recv()
        left = a2[k, p.x].astype(F32)
        for j in range(p.nx - 1):
            left = left + a3[j, k].astype(F32)
        right = b2[k, p.y].astype(F32)
        for j in range(p.ny - 1):
            right = right + b3[j, k].astype(F32)
        if k:
            a4[k - 1] = left.astype(BF16)
            b4[k - 1] = right.astype(BF16)
            third.append(copies.start(a4.at[k - 1], a5.at[k - 1], p.device(z=p.zk(k))))
            third.append(copies.start(b4.at[k - 1], b5.at[k - 1], p.device(z=p.zk(k))))
            return None
        return left, right

    n = len(order)
    for i in range(n):
        core_sum(i)
        if i >= 1:
            first_sum(i - 1)
        if i >= 2:
            second_sum(i - 2)
    first_sum(n - 1)
    second_sum(n - 2)
    left, right = second_sum(n - 1)
    left = left + mixed_ref[:, a]
    right = right + mixed_ref[:, b]
    for copy in third:
        copy.wait_recv()
    for k in range(p.nz - 1):
        left = left + a5[k].astype(F32)
        right = right + b5[k].astype(F32)
    out_ref[:, a] = left.astype(BF16)
    out_ref[:, b] = right.astype(BF16)
    copies.finish()


def expert_kernel(x_ref, gate_w_ref, up_w_ref, down_w_ref, gate_ref, out_ref, acc_ref):
    i, last = pl.program_id(1), pl.num_programs(1) - 1
    x = x_ref[:, : out_ref.shape[1]]
    gate_part = jnp.dot(x, gate_w_ref[...], preferred_element_type=F32)
    up_part = jnp.dot(x, up_w_ref[...], preferred_element_type=F32)
    act = (jax.nn.silu(gate_part) * up_part).astype(BF16)
    part = jnp.dot(act, down_w_ref[...], preferred_element_type=F32)

    @pl.when(i == 0)
    def _():
        acc_ref[...] = part

    @pl.when((i > 0) & (i < last))
    def _():
        acc_ref[...] += part

    @pl.when(i == last)
    def _():
        total = jnp.where(i > 0, acc_ref[...] + part, part)
        out_ref[...] = (total.astype(BF16).astype(F32) * gate_ref[...]).astype(BF16)


def local(
    queries, prefix_keys, prefix_values, suffix_keys, suffix_values, parents, out_proj,
    residual, norm_gain, router, routes, expert_gate, expert_up, expert_down,
):
    n_seq, n_grp = lax.axis_size("seq"), lax.axis_size("grp")
    nz, nx, ny = dims(n_seq, n_grp)
    s, g = lax.axis_index("seq"), lax.axis_index("grp")
    rows, width = queries.shape[1], queries.shape[2]
    total_rows = rows * n_seq
    keys = prefix_keys.shape[1]
    kv_width = suffix_keys.shape[2]
    group = HEADS // KVH
    own_heads = HEADS // n_seq
    own_width = own_heads * HD
    vmem = pltpu.VMEM

    packed = jnp.concatenate([queries[0], suffix_keys[0], suffix_values[0]], axis=1)
    pack_width = packed.shape[1]
    gathered = call(
        functools.partial(gather_kernel, n_seq, n_grp),
        jax.ShapeDtypeStruct((nz, nx, rows, pack_width), BF16),
        [packed], [], 0,
    ).reshape(total_rows, pack_width)

    o, m, l = pl.pallas_call(
        functools.partial(prefix_kernel, group),
        grid=(KVH,),
        in_specs=[
            pl.BlockSpec((total_rows, group * HD), lambda i: (0, i)),
            pl.BlockSpec((keys, HD), lambda i: (0, i)),
            pl.BlockSpec((keys, HD), lambda i: (0, i)),
        ],
        out_specs=[
            pl.BlockSpec((group * HD, total_rows), lambda i: (i, 0)),
            pl.BlockSpec((group, total_rows), lambda i: (i, 0)),
            pl.BlockSpec((group, total_rows), lambda i: (i, 0)),
        ],
        out_shape=[
            jax.ShapeDtypeStruct((HEADS * HD, total_rows), F32),
            jax.ShapeDtypeStruct((HEADS, total_rows), F32),
            jax.ShapeDtypeStruct((HEADS, total_rows), F32),
        ],
        compiler_params=pltpu.CompilerParams(vmem_limit_bytes=VLIMIT),
    )(gathered, prefix_keys[0], prefix_values[0])

    o_own, l_own, m_own = call(
        functools.partial(merge_kernel, n_seq, n_grp),
        [
            jax.ShapeDtypeStruct((own_width, total_rows), F32),
            jax.ShapeDtypeStruct((own_heads, total_rows), F32),
            jax.ShapeDtypeStruct((own_heads, total_rows), F32),
        ],
        [
            o.reshape(n_seq, own_width, total_rows),
            m.reshape(n_seq, own_heads, total_rows),
            l.reshape(n_seq, own_heads, total_rows),
        ],
        [
            vmem((n_seq, n_seq, own_heads, total_rows), F32),
            vmem((n_seq - 1, own_heads, total_rows), F32),
            vmem((n_seq, own_width, total_rows), BF16),
            vmem((nx - 1, nz, own_width, total_rows), BF16),
            vmem((nz - 1, own_width, total_rows), BF16),
            vmem((nz - 1, own_width, total_rows), BF16),
        ],
        1,
    )

    kv_index = s * own_heads // group
    own_q = lax.dynamic_slice_in_dim(gathered, s * own_width, own_width, 1)
    own_k = lax.dynamic_slice_in_dim(gathered, width + kv_index * HD, HD, 1)
    own_v = lax.dynamic_slice_in_dim(gathered, width + kv_width + kv_index * HD, HD, 1)
    tile = min(1024, width)
    whole = lambda *shape: pl.BlockSpec(shape, lambda i: (0,) * len(shape))
    projected = pl.pallas_call(
        functools.partial(project_kernel, own_heads),
        grid=(width // tile,),
        in_specs=[
            whole(total_rows, own_width), whole(total_rows, HD), whole(total_rows, HD),
            whole(1, total_rows), whole(own_width, total_rows), whole(own_heads, total_rows),
            whole(own_heads, total_rows), pl.BlockSpec((own_width, tile), lambda i: (0, i)),
        ],
        out_specs=pl.BlockSpec((total_rows, tile), lambda i: (0, i)),
        out_shape=jax.ShapeDtypeStruct((total_rows, width), BF16),
        scratch_shapes=[vmem((total_rows, own_width), BF16)],
        compiler_params=pltpu.CompilerParams(vmem_limit_bytes=VLIMIT),
    )(own_q, own_k, own_v, parents, o_own, l_own, m_own, out_proj)

    experts = router.shape[1]
    lanes = -(-2 * experts // 128) * 128
    chosen = jnp.sum(
        (routes[0][:, :, None] == jnp.arange(experts, dtype=jnp.int32)).astype(F32), axis=1
    )
    pad = ((0, 0), (0, lanes - 2 * experts))
    chosen = jnp.pad(jnp.concatenate([chosen, chosen], axis=1), pad)
    router_wide = jnp.pad(jnp.concatenate([router, router], axis=1), pad)
    mixed, arrived = call(
        functools.partial(norm_kernel, n_seq, n_grp, experts),
        [
            jax.ShapeDtypeStruct((rows, width), F32),
            jax.ShapeDtypeStruct((2, nz, nx, ny, rows, width + lanes), BF16),
        ],
        [
            projected.reshape(nz, nx, rows, width), residual[0], norm_gain[None], router_wide,
            chosen,
        ],
        [
            vmem((nx - 1, nz, rows, width), BF16),
            vmem((nz - 1, rows, width), BF16),
            vmem((nz - 1, rows, width), BF16),
        ],
        2,
    )

    flat = arrived.reshape(-1, width + lanes)
    parts = flat[:, width:].astype(F32)
    expert = s * n_grp + g
    lane = jnp.arange(lanes, dtype=jnp.int32)
    mine = (lane == expert) | (lane == expert + experts)
    gate = jnp.sum(jnp.where(mine[None, :], parts, 0.0), axis=1, keepdims=True)
    hidden = expert_gate.shape[2]
    row_tile, tile = min(512, flat.shape[0]), min(256, hidden)
    weighted = pl.pallas_call(
        expert_kernel,
        grid=(flat.shape[0] // row_tile, hidden // tile),
        in_specs=[
            pl.BlockSpec((row_tile, width + lanes), lambda r, i: (r, 0)),
            pl.BlockSpec((width, tile), lambda r, i: (0, i)),
            pl.BlockSpec((width, tile), lambda r, i: (0, i)),
            pl.BlockSpec((tile, width), lambda r, i: (i, 0)),
            pl.BlockSpec((row_tile, 1), lambda r, i: (r, 0)),
        ],
        out_specs=pl.BlockSpec((row_tile, width), lambda r, i: (r, 0)),
        out_shape=jax.ShapeDtypeStruct((flat.shape[0], width), BF16),
        scratch_shapes=[vmem((row_tile, width), F32)],
        compiler_params=pltpu.CompilerParams(vmem_limit_bytes=VLIMIT),
    )(flat, expert_gate[0], expert_up[0], expert_down[0], gate)

    half = width // 2
    out = call(
        functools.partial(combine_kernel, n_seq, n_grp),
        jax.ShapeDtypeStruct((rows, width), BF16),
        [weighted.reshape(2, nz, nx, ny, rows, width), mixed],
        [
            vmem((nz, nx, ny, rows, width), BF16),
            vmem((nz, nx, ny, rows, width), BF16),
            vmem((ny - 1, nz, nx, rows, half), BF16),
            vmem((nx - 1, nz, ny, rows, half), BF16),
            vmem((nz, nx, rows, half), BF16),
            vmem((nz, ny, rows, half), BF16),
            vmem((nx - 1, nz, rows, half), BF16),
            vmem((ny - 1, nz, rows, half), BF16),
            vmem((nz - 1, rows, half), BF16),
            vmem((nz - 1, rows, half), BF16),
            vmem((nz - 1, rows, half), BF16),
            vmem((nz - 1, rows, half), BF16),
        ],
        3,
    )
    return out[None]


def solution(mesh):
    in_specs = (
        P("grp", "seq", None),
        P("grp", "seq", None),
        P("grp", "seq", None),
        P("grp", "seq", None),
        P("grp", "seq", None),
        P("grp", None),
        P("seq", None),
        P("grp", "seq", None),
        P(),
        P(),
        P("grp", "seq", None),
        P(("seq", "grp"), None, None),
        P(("seq", "grp"), None, None),
        P(("seq", "grp"), None, None),
    )
    out_specs = P("grp", "seq", None)
    return jax.shard_map(local, mesh=mesh, in_specs=in_specs, out_specs=out_specs, check_vma=False)
```
